128 devices in a mesh: row: 16 (over y, z), col: 8 (over x, core).
Axes of the slice: x: 4, y: 4, z: 4, core: 2. Of those that a mesh axis runs over, the one named last changes fastest.
Arguments:
- amplitude: float32 [512, 256, 256], P(('row', 'col')), may hold values from 0.1 to 3
- patches: float32 [512, 2, 256, 256], P(('row', 'col')), may hold values from -5 to 5
- dual: float32 [512, 3, 2, 256, 256], P(('row', 'col')), may hold values from -3 to 3
- probe: float32 [3, 2, 256, 256], replicated, may hold values from -6 to 6
- obj: float32 [2, 12288, 6144], P(None, 'row', 'col'), may hold values from -5 to 5
- positions: int32 [512, 2], P(('row', 'col')), may hold values from 0 to 12032, as said below
Outputs:
- dual_new: float32 [512, 3, 2, 256, 256], P(('row', 'col'))
- object_new: float32 [2, 12288, 6144], P(None, 'row', 'col')
- probe_new: float32 [3, 2, 256, 256], replicated
- patches_new: float32 [512, 2, 256, 256], P(('row', 'col'))
The draws below stay inside these ranges and needn't reach their ends.
Inputs may be any that keep to these rules, and one draw needn't show every extreme that they name: `positions`: both entries of each row are multiples of 128. A frame held by the device at index i of row and j of col has its row offset between i * 768 and (i + 1) * 768 - 128 and its column offset between j * 768 and (j + 1) * 768 - 128; every frame lies inside the object.
All inputs are finite; a program needn't handle non-finite values.
Results may differ from the reference program's by a relative error of at most 0.0003.
Values sent between devices are 32-bit elements; how exact they have to be, the bound alone decides.
A program may use at most 192 MiB of HBM per device.

```python
import math
import jax
import jax.numpy as jnp
from jax import lax

FRAME = 256
MODES = 3
FR_DEV = 4
TILE = 768
SWEEPS = 4
FRAMES = 512
OBJ_ROWS = 12288
OBJ_COLS = 6144


def draw_positions(key, part):
    frame_ids = jnp.arange(FRAMES, dtype=jnp.int32)
    device_ids = frame_ids // FR_DEV
    tile_cols = OBJ_COLS // TILE
    tile_rows = OBJ_ROWS // TILE
    grid_row = device_ids // tile_cols
    grid_col = device_ids % tile_cols
    step_size = FRAME // 2
    places = TILE // step_size
    top_row = jnp.where(grid_row == tile_rows - 1, places - 1, places)
    top_col = jnp.where(grid_col == tile_cols - 1, places - 1, places)
    key_rows = jax.random.fold_in(key, 11)
    key_cols = jax.random.fold_in(key, 23)
    offset_row = jax.random.randint(key_rows, (FRAMES,), 0, top_row, dtype=jnp.int32)
    offset_col = jax.random.randint(key_cols, (FRAMES,), 0, top_col, dtype=jnp.int32)
    first = grid_row * TILE + offset_row * step_size
    second = grid_col * TILE + offset_col * step_size
    return jnp.stack([first, second], axis=1).astype(jnp.int32)


def steps_of(stream_key, dims, pieces, least, largest):
    factor_of = 1.0
    for position, parts in pieces:
        heights = jax.random.uniform(jax.random.fold_in(jax.random.fold_in(stream_key, 6), position), (parts,), jnp.float32, least / len(pieces), largest / len(pieces))
        factor_of = factor_of * jnp.repeat(jnp.exp(heights), dims[position] // parts).reshape((-1,) + (1,) * (len(dims) - 1 - position))
    return factor_of


def gaussian(rng, extent, scale, most, cuts=(), kind=jnp.bfloat16):
    entries = jax.random.normal(rng, extent, jnp.float32) * scale
    if len(cuts) > 0:
        entries = steps_of(rng, extent, cuts, -0.22, 0.18) * entries
    return jnp.clip(entries, min=-most, max=most).astype(kind)


def setup_inputs(seed: int = 0) -> dict:
    streams_of = jax.random.split(jax.random.key(seed), 7)
    return {
        "amplitude": jnp.clip(jnp.exp(math.log(3.0) - 3.4011974 * jax.random.uniform(streams_of[0], (FRAMES, FRAME, FRAME), jnp.float32) ** steps_of(streams_of[0], (FRAMES, FRAME, FRAME), ((0, 128),), -0.2, 0.2)), 0.1, 3.0),
        "patches": gaussian(streams_of[1], (FRAMES, 2, FRAME, FRAME), 0.7, 5.0, ((0, 128),), jnp.float32),
        "dual": gaussian(streams_of[2], (FRAMES, MODES, 2, FRAME, FRAME), 0.3, 3.0, ((0, 128),), jnp.float32),
        "probe": gaussian(streams_of[3], (MODES, 2, FRAME, FRAME), 1.0, 6.0, (), jnp.float32),
        "obj": gaussian(streams_of[4], (2, OBJ_ROWS, OBJ_COLS), 0.7, 5.0, ((1, 16), (2, 8)), jnp.float32),
        "positions": draw_positions(jax.random.fold_in(streams_of[6], 71), 0),
    }


amp_floor = 1.0
obj_weight = 0.5
smooth_weight = 16.0
probe_weight = 1.0

def tables(width):
    index = jnp.arange(width, dtype=jnp.int32)
    product = index[:, None] * index[None, :] % width
    angle = product.astype(jnp.float32) * (2.0 * math.pi / width)
    scaling = 1.0 / math.sqrt(width)
    return (jnp.cos(angle) * scaling, jnp.sin(angle) * scaling)

def dft_pair(real_part, imag_part, cos_tab, sin_tab):
    highest = lax.Precision.HIGHEST
    left_re = jnp.matmul(cos_tab, real_part, precision=highest) - jnp.matmul(sin_tab, imag_part, precision=highest)
    left_im = jnp.matmul(cos_tab, imag_part, precision=highest) + jnp.matmul(sin_tab, real_part, precision=highest)
    out_re = jnp.matmul(left_re, cos_tab, precision=highest) - jnp.matmul(left_im, sin_tab, precision=highest)
    out_im = jnp.matmul(left_re, sin_tab, precision=highest) + jnp.matmul(left_im, cos_tab, precision=highest)
    return (out_re, out_im)

def frame_update(amplitude, patches, dual, probe, cos_tab, sin_tab):
    patch_re = patches[:, 0][:, None]
    patch_im = patches[:, 1][:, None]
    probe_re = probe[:, 0]
    probe_im = probe[:, 1]
    exit_re = probe_re * patch_re - probe_im * patch_im
    exit_im = probe_re * patch_im + probe_im * patch_re
    dual_re = dual[:, :, 0]
    dual_im = dual[:, :, 1]
    far_re, far_im = dft_pair(exit_re + dual_re, exit_im + dual_im, cos_tab, -sin_tab)
    intensity = lax.optimization_barrier(jnp.sum(far_re * far_re + far_im * far_im, axis=1))
    ratio = (amplitude / jnp.sqrt(intensity + amp_floor))[:, None]
    near_re, near_im = dft_pair(far_re * ratio, far_im * ratio, cos_tab, sin_tab)
    new_re = dual_re + exit_re - near_re
    new_im = dual_im + exit_im - near_im
    return (new_re, new_im, near_re - new_re, near_im - new_im)

def reference(amplitude, patches, dual, probe, obj, positions):
    cos_tab, sin_tab = tables(FRAME)
    probe_re = probe[:, 0]
    probe_im = probe[:, 1]
    probe_power = lax.optimization_barrier(jnp.sum(probe_re * probe_re + probe_im * probe_im, axis=0))

    def advance(carry, item):
        canvas, probe_num, probe_den = carry
        amp_one, patch_one, dual_one, place = item
        new_re, new_im, target_re, target_im = frame_update(amp_one[None], patch_one[None], dual_one[None], probe, cos_tab, sin_tab)
        new_re, new_im, target_re, target_im = (new_re[0], new_im[0], target_re[0], target_im[0])
        patch_re = patch_one[0]
        patch_im = patch_one[1]
        probe_num = probe_num + jnp.stack([patch_re * target_re + patch_im * target_im, patch_re * target_im - patch_im * target_re], axis=1)
        probe_den = probe_den + patch_re * patch_re + patch_im * patch_im
        obj_re = lax.optimization_barrier(jnp.sum(probe_re * target_re + probe_im * target_im, axis=0))
        obj_im = lax.optimization_barrier(jnp.sum(probe_re * target_im - probe_im * target_re, axis=0))
        contrib = jnp.stack([obj_re, obj_im, probe_power])
        start = (jnp.zeros((), jnp.int32), place[0].astype(jnp.int32), place[1].astype(jnp.int32))
        current = lax.dynamic_slice(canvas, start, (3, FRAME, FRAME))
        canvas = lax.dynamic_update_slice(canvas, current + contrib, start)
        return ((canvas, probe_num, probe_den), jnp.stack([new_re, new_im], axis=1))
    init = (jnp.zeros((3, OBJ_ROWS, OBJ_COLS), jnp.float32), jnp.zeros((MODES, 2, FRAME, FRAME), jnp.float32), jnp.zeros((FRAME, FRAME), jnp.float32))
    (canvas, probe_num, probe_den), dual_new = lax.scan(advance, init, (amplitude, patches, dual, positions))
    probe_new = (probe_num + probe_weight * probe) / (probe_den + probe_weight)
    rhs = canvas[:2] + obj_weight * obj
    diagonal = canvas[2] + obj_weight + 4.0 * smooth_weight
    field = obj
    for sweep in range(SWEEPS):
        padded = jnp.pad(field, ((0, 0), (1, 1), (1, 1)))
        beside = padded[:, 2:, 1:-1] + padded[:, :-2, 1:-1] + padded[:, 1:-1, 2:] + padded[:, 1:-1, :-2]
        field = (rhs + smooth_weight * beside) / diagonal

    def window(place):
        start = (jnp.zeros((), jnp.int32), place[0].astype(jnp.int32), place[1].astype(jnp.int32))
        return lax.dynamic_slice(field, start, (2, FRAME, FRAME))
    patches_new = lax.map(window, positions)
    return (dual_new, field, probe_new, patches_new)
```

```python
import math
import numpy as np
import ml_dtypes
import jax
import jax.numpy as jnp
from jax import lax
from jax.experimental import pallas as pl
from jax.experimental.pallas import tpu as pltpu
from jax.sharding import PartitionSpec as P

N = 256
H = 128
MODES = 3
TILE = 768
WIDE = TILE + H
F32, BF16 = jnp.float32, jnp.bfloat16


def dft_tables():
    k = np.arange(H)
    stacked = []
    for odd in (0, 1):
        angle = ((2 * k[:, None] + odd) * k[None, :] % N) * (2.0 * math.pi / N)
        c, s = np.cos(angle) / 16.0, np.sin(angle) / 16.0
        stacked.append(np.block([[c, s], [-s, c]]))
    whole = np.stack(stacked + [t.T for t in stacked]).astype(np.float32)
    lead = whole.astype(ml_dtypes.bfloat16)
    rest = (whole - lead.astype(np.float32)).astype(ml_dtypes.bfloat16)
    return np.stack([lead, rest], axis=1)


def order_table():
    t = np.zeros((N, N), np.float32)
    k = np.arange(H)
    t[2 * k, k] = 1.0
    t[2 * k + 1, H + k] = 1.0
    return np.stack([t, t.T]).astype(ml_dtypes.bfloat16)


def parts(x):
    lead = x.astype(BF16)
    return lead, (x - lead.astype(F32)).astype(BF16)


def dot(a, b):
    return lax.dot_general(a, b, (((1,), (0,)), ((), ())), preferred_element_type=F32)


def left(tab, which, x):
    lead, rest = parts(x)
    a, b = tab[which, 0], tab[which, 1]
    return dot(jnp.concatenate([a, a, b], axis=1), jnp.concatenate([lead, rest, lead], axis=0))


def right(tab, which, x):
    lead, rest = parts(x)
    a, b = tab[which, 0], tab[which, 1]
    return dot(jnp.concatenate([lead, rest, lead], axis=1), jnp.concatenate([a, a, b], axis=0))


def top(x):
    return x[:H]


def bot(x):
    return x[H:]


def lft(x):
    return x[:, :H]


def rgt(x):
    return x[:, H:]


def rows2(a, b):
    return jnp.concatenate([a, b], axis=0)


def cols2(a, b):
    return jnp.concatenate([a, b], axis=1)


def forward(tab, xr, xi):
    e = left(tab, 0, rows2(top(xr) + bot(xr), top(xi) + bot(xi)))
    o = left(tab, 1, rows2(top(xr) - bot(xr), top(xi) - bot(xi)))
    yr, yi = rows2(top(e), top(o)), rows2(bot(e), bot(o))
    even = right(tab, 2, cols2(lft(yr) + rgt(yr), lft(yi) + rgt(yi)))
    odd = right(tab, 3, cols2(lft(yr) - rgt(yr), lft(yi) - rgt(yi)))
    return even, odd


def inverse(tab, even, odd):
    a = right(tab, 0, even)
    b = right(tab, 1, odd)
    yr = cols2(lft(a) + lft(b), lft(a) - lft(b))
    yi = cols2(rgt(a) + rgt(b), rgt(a) - rgt(b))
    e = left(tab, 2, rows2(top(yr), top(yi)))
    o = left(tab, 3, rows2(bot(yr), bot(yi)))
    xr = rows2(top(e) + top(o), top(e) - top(o))
    xi = rows2(bot(e) + bot(o), bot(e) - bot(o))
    return xr, xi


def frame_kernel(place, amp, patches, dual, probe, tab, order, dual_new, canvas, sums, far):
    f = pl.program_id(0)

    @pl.when(f == 0)
    def _():
        canvas[...] = jnp.zeros_like(canvas)
        sums[...] = jnp.zeros_like(sums)

    pr, pi = patches[0, 0], patches[0, 1]
    sums[6] += pr * pr + pi * pi
    power_e = power_o = None
    for m in range(MODES):
        qr, qi = probe[m, 0], probe[m, 1]
        xr = qr * pr - qi * pi + dual[0, m, 0]
        xi = qr * pi + qi * pr + dual[0, m, 1]
        even, odd = forward(tab, xr, xi)
        far[m, 0] = even
        far[m, 1] = odd
        e2 = lft(even) * lft(even) + rgt(even) * rgt(even)
        o2 = lft(odd) * lft(odd) + rgt(odd) * rgt(odd)
        power_e = e2 if power_e is None else power_e + e2
        power_o = o2 if power_o is None else power_o + o2
    lead, rest = parts(amp[0])
    a = dot(cols2(order[1], order[1]), rows2(lead, rest))
    lead, rest = parts(a)
    a = dot(cols2(lead, rest), rows2(order[0], order[0]))
    ratio_e = lft(a) * lax.rsqrt(power_e + 1.0)
    ratio_o = rgt(a) * lax.rsqrt(power_o + 1.0)
    ratio_e, ratio_o = cols2(ratio_e, ratio_e), cols2(ratio_o, ratio_o)
    obj_re = obj_im = None
    for m in range(MODES):
        qr, qi = probe[m, 0], probe[m, 1]
        nr, ni = inverse(tab, far[m, 0] * ratio_e, far[m, 1] * ratio_o)
        dr = dual[0, m, 0] + (qr * pr - qi * pi) - nr
        di = dual[0, m, 1] + (qr * pi + qi * pr) - ni
        dual_new[0, m, 0] = dr
        dual_new[0, m, 1] = di
        tr, ti = nr - dr, ni - di
        sums[2 * m] += pr * tr + pi * ti
        sums[2 * m + 1] += pr * ti - pi * tr
        re = qr * tr + qi * ti
        im = qr * ti - qi * tr
        obj_re = re if obj_re is None else obj_re + re
        obj_im = im if obj_im is None else obj_im + im
    r = pl.multiple_of(place[f, 0], H)
    c = pl.multiple_of(place[f, 1], H)
    canvas[0, pl.ds(r, N), pl.ds(c, N)] += obj_re
    canvas[1, pl.ds(r, N), pl.ds(c, N)] += obj_im
    square = probe[...] * probe[...]
    canvas[2, pl.ds(r, N), pl.ds(c, N)] += jnp.sum(square, axis=(0, 1))


def frames(place, amp, patches, dual, probe):
    n = amp.shape[0]
    tab, order = jnp.asarray(dft_tables()), jnp.asarray(order_table())
    whole = lambda *d: pl.BlockSpec(d, lambda f, p: (0,) * len(d))
    grid = pltpu.PrefetchScalarGridSpec(
        num_scalar_prefetch=1,
        grid=(n,),
        in_specs=[
            pl.BlockSpec((1, N, N), lambda f, p: (f, 0, 0)),
            pl.BlockSpec((1, 2, N, N), lambda f, p: (f, 0, 0, 0)),
            pl.BlockSpec((1, MODES, 2, N, N), lambda f, p: (f, 0, 0, 0, 0)),
            whole(MODES, 2, N, N),
            whole(4, 2, N, N),
            whole(2, N, N),
        ],
        out_specs=[
            pl.BlockSpec((1, MODES, 2, N, N), lambda f, p: (f, 0, 0, 0, 0)),
            whole(3, WIDE, WIDE),
            whole(7, N, N),
        ],
        scratch_shapes=[pltpu.VMEM((MODES, 2, N, N), F32)],
    )
    return pl.pallas_call(
        frame_kernel,
        grid_spec=grid,
        out_shape=[
            jax.ShapeDtypeStruct(dual.shape, F32),
            jax.ShapeDtypeStruct((3, WIDE, WIDE), F32),
            jax.ShapeDtypeStruct((7, N, N), F32),
        ],
        compiler_params=pltpu.CompilerParams(vmem_limit_bytes=56 << 20),
    )(place, amp, patches, dual, probe, tab, order)


SWEEPS = 4


amp_floor = 1.0
obj_weight = 0.5
smooth_weight = 16.0
probe_weight = 1.0


def from_behind(block, axis, distance):
    devices = range(lax.axis_size(axis))
    route = [(i - distance, i) for i in devices if i - distance in devices]
    return lax.ppermute(block, axis, route)


def extended_2(block, sides, width):
    for axis, dim in sides:
        count = lax.axis_size(axis)
        forward = [(i, i + 1) for i in range(count - 1)]
        backward = [(target, source) for source, target in forward]
        low = lax.ppermute(
            lax.slice_in_dim(block, block.shape[dim] - width, None, axis=dim), axis, forward
        )
        high = lax.ppermute(lax.slice_in_dim(block, 0, width, axis=dim), axis, backward)
        block = jnp.concatenate([low, block, high], axis=dim)
    return block


def neighbours(padded):
    return padded[:, 2:, 1:-1] + padded[:, :-2, 1:-1] + padded[:, 1:-1, 2:] + padded[:, 1:-1, :-2]


def per_device(amplitude, patches, dual, probe, obj, positions):
    width = amplitude.shape[-1]
    half_width = width // 2
    modes = probe.shape[0]
    tile = obj.shape[1]
    row_index = lax.axis_index("row")
    col_index = lax.axis_index("col")
    origin = jnp.stack([row_index, col_index]).astype(jnp.int32) * tile
    place = positions - origin
    dual_new, canvas, sums = frames(place, amplitude, patches, dual, probe)
    packed = sums.reshape(7, width * width)
    probe_flat = probe.reshape(2 * modes, width * width)
    totals = lax.psum(packed, ("row", "col"))
    probe_new = (
        (totals[: 2 * modes] + probe_weight * probe_flat) / (totals[2 * modes :] + probe_weight)
    ).reshape(probe.shape)
    local_rows = place[:, 0]
    local_cols = place[:, 1]
    anchor = jnp.zeros((), jnp.int32)

    from_left = from_behind(canvas[:, :, tile:], "col", 1)
    canvas = canvas.at[:, :, :half_width].add(from_left)
    from_above = from_behind(canvas[:, tile:, :tile], "row", 1)
    sums_own = canvas[:, :tile, :tile].at[:, :half_width, :].add(from_above)
    rhs = sums_own[:2] + obj_weight * obj
    diagonal = sums_own[2] + obj_weight + 4.0 * smooth_weight
    field = obj
    for sweep in range(SWEEPS):
        padded = extended_2(field, (("row", 1), ("col", 2)), 1)
        field = (rhs + smooth_weight * neighbours(padded)) / diagonal
    from_right = from_behind(field[:, :, :half_width], "col", -1)
    wider = jnp.concatenate([field, from_right], axis=2)
    from_below = from_behind(wider[:, :half_width, :], "row", -1)
    extended = jnp.concatenate([wider, from_below], axis=1)

    def window(row_start, col_start):
        return lax.dynamic_slice(extended, (anchor, row_start, col_start), (2, width, width))

    patches_new = jax.vmap(window)(local_rows, local_cols)
    return (dual_new, field, probe_new, patches_new)


def solution(mesh):
    return jax.shard_map(
        per_device,
        mesh=mesh,
        in_specs=(
            P(("row", "col"), None, None),
            P(("row", "col"), None, None, None),
            P(("row", "col"), None, None, None, None),
            P(),
            P(None, "row", "col"),
            P(("row", "col"), None),
        ),
        out_specs=(
            P(("row", "col"), None, None, None, None),
            P(None, "row", "col"),
            P(),
            P(("row", "col"), None, None, None),
        ),
        check_vma=False,
    )
```

```python
import math
import numpy as np
import ml_dtypes
import jax
import jax.numpy as jnp
from jax import lax
from jax.experimental import pallas as pl
from jax.experimental.pallas import tpu as pltpu
from jax.sharding import PartitionSpec as P

N = 256
H = 128
MODES = 3
TILE = 768
WIDE = TILE + H
TILES = 8
ROWS = 904
BAND = 136
LOW = TILE - 8
MESH = pl.DeviceIdType.MESH
F32, BF16 = jnp.float32, jnp.bfloat16


def dft_tables():
    k = np.arange(H)
    stacked = []
    for odd in (0, 1):
        angle = ((2 * k[:, None] + odd) * k[None, :] % N) * (2.0 * math.pi / N)
        c, s = np.cos(angle) / 16.0, np.sin(angle) / 16.0
        stacked.append(np.block([[c, s], [-s, c]]))
    whole = np.stack(stacked + [t.T for t in stacked]).astype(np.float32)
    lead = whole.astype(ml_dtypes.bfloat16)
    rest = (whole - lead.astype(np.float32)).astype(ml_dtypes.bfloat16)
    return np.stack([lead, rest], axis=1)


def order_table():
    t = np.zeros((N, N), np.float32)
    k = np.arange(H)
    t[2 * k, k] = 1.0
    t[2 * k + 1, H + k] = 1.0
    return np.stack([t, t.T]).astype(ml_dtypes.bfloat16)


def parts(x):
    lead = x.astype(BF16)
    return lead, (x - lead.astype(F32)).astype(BF16)


def dot(a, b):
    return lax.dot_general(a, b, (((1,), (0,)), ((), ())), preferred_element_type=F32)


def left(tab, which, x):
    lead, rest = parts(x)
    a, b = tab[which, 0], tab[which, 1]
    return dot(jnp.concatenate([a, a, b], axis=1), jnp.concatenate([lead, rest, lead], axis=0))


def right(tab, which, x):
    lead, rest = parts(x)
    a, b = tab[which, 0], tab[which, 1]
    return dot(jnp.concatenate([lead, rest, lead], axis=1), jnp.concatenate([a, a, b], axis=0))


def top(x):
    return x[:H]


def bot(x):
    return x[H:]


def lft(x):
    return x[:, :H]


def rgt(x):
    return x[:, H:]


def rows2(a, b):
    return jnp.concatenate([a, b], axis=0)


def cols2(a, b):
    return jnp.concatenate([a, b], axis=1)


def forward(tab, xr, xi):
    e = left(tab, 0, rows2(top(xr) + bot(xr), top(xi) + bot(xi)))
    o = left(tab, 1, rows2(top(xr) - bot(xr), top(xi) - bot(xi)))
    yr, yi = rows2(top(e), top(o)), rows2(bot(e), bot(o))
    even = right(tab, 2, cols2(lft(yr) + rgt(yr), lft(yi) + rgt(yi)))
    odd = right(tab, 3, cols2(lft(yr) - rgt(yr), lft(yi) - rgt(yi)))
    return even, odd


def inverse(tab, even, odd):
    a = right(tab, 0, even)
    b = right(tab, 1, odd)
    yr = cols2(lft(a) + lft(b), lft(a) - lft(b))
    yi = cols2(rgt(a) + rgt(b), rgt(a) - rgt(b))
    e = left(tab, 2, rows2(top(yr), top(yi)))
    o = left(tab, 3, rows2(bot(yr), bot(yi)))
    xr = rows2(top(e) + top(o), top(e) - top(o))
    xi = rows2(bot(e) + bot(o), bot(e) - bot(o))
    return xr, xi


def frame_kernel(place, amp, patches, dual, probe, tab, order, dual_new, canvas, sums, count, far):
    f = pl.program_id(0)

    @pl.when(f == 0)
    def _():
        canvas[...] = jnp.zeros_like(canvas)
        sums[...] = jnp.zeros_like(sums)
        count[...] = jnp.zeros_like(count)

    pr, pi = patches[0, 0], patches[0, 1]
    sums[6] += pr * pr + pi * pi
    power_e = power_o = None
    for m in range(MODES):
        qr, qi = probe[m, 0], probe[m, 1]
        xr = qr * pr - qi * pi + dual[0, m, 0]
        xi = qr * pi + qi * pr + dual[0, m, 1]
        even, odd = forward(tab, xr, xi)
        far[m, 0] = even
        far[m, 1] = odd
        e2 = lft(even) * lft(even) + rgt(even) * rgt(even)
        o2 = lft(odd) * lft(odd) + rgt(odd) * rgt(odd)
        power_e = e2 if power_e is None else power_e + e2
        power_o = o2 if power_o is None else power_o + o2
    lead, rest = parts(amp[0])
    a = dot(cols2(order[1], order[1]), rows2(lead, rest))
    lead, rest = parts(a)
    a = dot(cols2(lead, rest), rows2(order[0], order[0]))
    ratio_e = lft(a) * lax.rsqrt(power_e + 1.0)
    ratio_o = rgt(a) * lax.rsqrt(power_o + 1.0)
    ratio_e, ratio_o = cols2(ratio_e, ratio_e), cols2(ratio_o, ratio_o)
    obj_re = obj_im = None
    for m in range(MODES):
        qr, qi = probe[m, 0], probe[m, 1]
        nr, ni = inverse(tab, far[m, 0] * ratio_e, far[m, 1] * ratio_o)
        dr = dual[0, m, 0] + (qr * pr - qi * pi) - nr
        di = dual[0, m, 1] + (qr * pi + qi * pr) - ni
        dual_new[0, m, 0] = dr
        dual_new[0, m, 1] = di
        tr, ti = nr - dr, ni - di
        sums[2 * m] += pr * tr + pi * ti
        sums[2 * m + 1] += pr * ti - pi * tr
        re = qr * tr + qi * ti
        im = qr * ti - qi * tr
        obj_re = re if obj_re is None else obj_re + re
        obj_im = im if obj_im is None else obj_im + im
    r = pl.multiple_of(place[f, 0], H)
    c = place[f, 1] // H
    for p, value in enumerate((obj_re, obj_im)):
        canvas[p, c, pl.ds(r, N)] += lft(value)
        canvas[p, c + 1, pl.ds(r, N)] += rgt(value)
    line = lax.broadcasted_iota(jnp.int32, (8, H), 0)
    lane = lax.broadcasted_iota(jnp.int32, (8, H), 1)
    count[...] += jnp.where((line == place[f, 0] // H) & (lane == c), 1.0, 0.0)


def frames(place, amp, patches, dual, probe):
    n = amp.shape[0]
    tab, order = jnp.asarray(dft_tables()), jnp.asarray(order_table())
    whole = lambda *d: pl.BlockSpec(d, lambda f, p: (0,) * len(d))
    grid = pltpu.PrefetchScalarGridSpec(
        num_scalar_prefetch=1,
        grid=(n,),
        in_specs=[
            pl.BlockSpec((1, N, N), lambda f, p: (f, 0, 0)),
            pl.BlockSpec((1, 2, N, N), lambda f, p: (f, 0, 0, 0)),
            pl.BlockSpec((1, MODES, 2, N, N), lambda f, p: (f, 0, 0, 0, 0)),
            whole(MODES, 2, N, N),
            whole(4, 2, N, N),
            whole(2, N, N),
        ],
        out_specs=[
            pl.BlockSpec((1, MODES, 2, N, N), lambda f, p: (f, 0, 0, 0, 0)),
            whole(2, TILES, ROWS, H),
            whole(7, N, N),
            whole(8, H),
        ],
        scratch_shapes=[pltpu.VMEM((MODES, 2, N, N), F32)],
    )
    return pl.pallas_call(
        frame_kernel,
        grid_spec=grid,
        out_shape=[
            jax.ShapeDtypeStruct(dual.shape, F32),
            jax.ShapeDtypeStruct((2, TILES, ROWS, H), F32),
            jax.ShapeDtypeStruct((7, N, N), F32),
            jax.ShapeDtypeStruct((8, H), F32),
        ],
        compiler_params=pltpu.CompilerParams(vmem_limit_bytes=56 << 20),
    )(place, amp, patches, dual, probe, tab, order)


def exchange_kernel(canvas, obj, sums, probe, count, cl, cr, bu, bd, ol, orr, ou, od, window, probe_new,
                    band_t, band_b, oband_t, oband_b, pair_in, half, y_in, quarter, x_in, chunk, z_all,
                    cnt_l, cnt_r, cnt_a, cnt_u, cnt_d, load_sem, send_sem, recv_sem):
    i, j = lax.axis_index("row"), lax.axis_index("col")
    y, z, x, core = i // 4, i % 4, j // 2, j % 2
    up, down = ((i + 15) % 16, j), ((i + 1) % 16, j)
    lf, rt = (i, (j + 7) % 8), (i, (j + 1) % 8)
    twin = (i, x * 2 + 1 - core)
    ys = [(((y + d) % 4) * 4 + z, j) for d in (1, 2, 3)]
    xs = [(i, ((x + d) % 4) * 2 + core) for d in (1, 2, 3)]
    zs = [(y * 4 + (z + d) % 4, j) for d in (1, 2, 3)]
    peers = [up, down, lf, rt, twin] + ys + xs + zs

    loads = [
        pltpu.make_async_copy(canvas.at[:, :, pl.ds(0, BAND)], band_t, load_sem.at[0]),
        pltpu.make_async_copy(canvas.at[:, :, pl.ds(LOW, BAND)], band_b, load_sem.at[1]),
    ]
    for t in range(6):
        lanes = pl.ds(H * t, H)
        loads.append(pltpu.make_async_copy(obj.at[:, pl.ds(0, BAND), lanes], oband_t.at[:, t], load_sem.at[2 + t]))
        loads.append(pltpu.make_async_copy(obj.at[:, pl.ds(LOW, 8), lanes], oband_b.at[:, t], load_sem.at[8 + t]))
    for c in loads:
        c.start()

    barrier = pltpu.get_barrier_semaphore()
    for p in peers:
        pl.semaphore_signal(barrier, inc=1, device_id=p, device_id_type=MESH)
    pl.semaphore_wait(barrier, len(peers))

    used = [0]
    started = []

    def send(src, dst, to):
        k = used[0]
        used[0] += 1
        c = pltpu.make_async_remote_copy(
            src_ref=src, dst_ref=dst, send_sem=send_sem.at[k], recv_sem=recv_sem.at[k],
            device_id=to, device_id_type=MESH,
        )
        c.start()
        started.append(c)
        return c

    def landed(*copies):
        for c in copies:
            c.wait_recv()

    other = pl.ds(pl.multiple_of((1 - core) * H, H), H)
    mine = pl.ds(pl.multiple_of(core * H, H), H)
    a_pair = send(sums.at[:, other], pair_in, twin)

    cols = []
    for r, n in ((0, BAND), (LOW, BAND)):
        rows = pl.ds(r, n)
        cols.append(send(canvas.at[:, pl.ds(5, 2), rows], cl.at[:, :, rows], rt))
        cols.append(send(canvas.at[:, pl.ds(0, 2), rows], cr.at[:, :, rows], lf))
    for r, n in ((0, BAND), (LOW, 8)):
        rows = pl.ds(r, n)
        cols.append(send(obj.at[:, rows, pl.ds(5 * H, H)], ol.at[:, rows], rt))
        cols.append(send(obj.at[:, rows, pl.ds(0, H)], orr.at[:, 0, rows], lf))
        cols.append(send(obj.at[:, rows, pl.ds(H, H)], orr.at[:, 1, rows], lf))
    cols.append(send(count, cnt_l, rt))
    cols.append(send(count, cnt_r, lf))

    landed(a_pair)
    half[...] = sums[:, mine] + pair_in[...]
    a_y = []
    for d in (1, 2, 3):
        rows = pl.ds(pl.multiple_of(((y + d) % 4) * 32, 32), 32)
        a_y.append(send(half.at[:, rows], y_in.at[d - 1], ys[d - 1]))

    landed(*cols)
    for c in loads:
        c.wait()
    lane = lax.broadcasted_iota(jnp.int32, (1, 8, H), 2)

    def edge(from_right, from_left):
        return jnp.where(lane < 4, from_right, jnp.where(lane >= H - 4, from_left, 0.0))

    def widen(first, band, oband, orows):
        def step(g, carry):
            at, src = pl.ds(pl.multiple_of(g * 8, 8), 8), pl.ds(pl.multiple_of(first + g * 8, 8), 8)
            band[:, 0, at] += cl[:, 1, src]
            band[:, 6, at] += cr[:, 0, src]
            band[:, 7, at] = edge(cr[:, 1, src], cl[:, 0, src])
            return carry

        def ostep(g, carry):
            at, src = pl.ds(pl.multiple_of(g * 8, 8), 8), pl.ds(pl.multiple_of(first + g * 8, 8), 8)
            oband[:, 6, at] = orr[:, 0, src]
            oband[:, 7, at] = edge(orr[:, 1, src], ol[:, src])
            return carry

        lax.fori_loop(0, BAND // 8, step, 0)
        lax.fori_loop(0, orows // 8, ostep, 0)

    widen(0, band_t, oband_t, BAND)
    widen(LOW, band_b, oband_b, 8)
    lane2 = lax.broadcasted_iota(jnp.int32, (8, H), 1)
    cnt_a[...] = jnp.where(
        lane2 < 2, pltpu.roll(cnt_l[...], H - 4, 1),
        jnp.where(lane2 < 8, pltpu.roll(count[...], 2, 1), jnp.where(lane2 < 10, pltpu.roll(cnt_r[...], 8, 1), 0.0)),
    )
    rows_ = [
        send(band_t, bd, up),
        send(band_b, bu, down),
        send(cnt_a, cnt_d, up),
        send(cnt_a, cnt_u, down),
        send(oband_t, od, up),
        send(oband_b, ou, down),
    ]
    rest = pl.ds(BAND, LOW - BAND)
    rows_ += [
        send(canvas.at[:, pl.ds(5, 2), rest], cl.at[:, :, rest], rt),
        send(canvas.at[:, pl.ds(0, 2), rest], cr.at[:, :, rest], lf),
        send(obj.at[:, rest, pl.ds(5 * H, H)], ol.at[:, rest], rt),
        send(obj.at[:, rest, pl.ds(0, H)], orr.at[:, 0, rest], lf),
        send(obj.at[:, rest, pl.ds(H, H)], orr.at[:, 1, rest], lf),
    ]

    landed(*a_y)
    rows = pl.ds(pl.multiple_of(y * 32, 32), 32)
    quarter[...] = half[:, rows] + y_in[0] + y_in[1] + y_in[2]
    a_x = []
    for d in (1, 2, 3):
        rows = pl.ds(pl.multiple_of(((x + d) % 4) * 8, 8), 8)
        a_x.append(send(quarter.at[:, rows], x_in.at[d - 1], xs[d - 1]))
    landed(*a_x)
    rows = pl.ds(pl.multiple_of(x * 8, 8), 8)
    chunk[...] = quarter[:, rows] + x_in[0] + x_in[1] + x_in[2]
    z_all[pl.ds(z, 1)] = chunk[...][None]
    a_z = [send(chunk, z_all.at[z], to) for to in zs]
    landed(*a_z)
    total = z_all[0] + z_all[1] + z_all[2] + z_all[3]
    at8 = pl.ds(pl.multiple_of(core * H + y * 32 + x * 8, 8), 8)
    at32 = pl.ds(pl.multiple_of(core * H + y * 32, 32), 32)
    probe_new[:, at8] = (total[:6] + probe[:, at8]) / (total[6:] + 1.0)
    landed(*[send(probe_new.at[:, at8], probe_new.at[:, at8], to) for to in xs])
    landed(*[send(probe_new.at[:, at32], probe_new.at[:, at32], to) for to in ys])
    at128 = pl.ds(pl.multiple_of(core * H, H), H)
    landed(send(probe_new.at[:, at128], probe_new.at[:, at128], twin))

    landed(*rows_)
    line = lax.broadcasted_iota(jnp.int32, (8, H), 0)
    above, own, below = pltpu.roll(cnt_u[...], 4, 0), pltpu.roll(cnt_a[...], 2, 0), cnt_d[...]
    window[pl.ds(0, 8)] = jnp.where(line < 2, above, own)
    window[pl.ds(8, 8)] = jnp.where(line < 2, below, 0.0)
    for c in started:
        c.wait_send()


def exchange(canvas, obj, sums, probe, count):
    f32 = lambda *d: jax.ShapeDtypeStruct(d, F32)
    vm, any_ = pl.BlockSpec(memory_space=pltpu.VMEM), pl.BlockSpec(memory_space=pl.ANY)
    v = lambda *d: pltpu.VMEM(d, F32)
    return pl.pallas_call(
        exchange_kernel,
        out_shape=[
            f32(2, 2, WIDE, H), f32(2, 2, WIDE, H), f32(2, TILES, BAND, H), f32(2, TILES, BAND, H),
            f32(2, TILE, H), f32(2, 2, TILE, H), f32(2, TILES, 8, H), f32(2, TILES, BAND, H),
            f32(16, H), f32(6, N, N),
        ],
        in_specs=[any_, any_, vm, vm, vm],
        out_specs=[vm] * 10,
        scratch_shapes=[
            v(2, TILES, BAND, H), v(2, TILES, BAND, H), v(2, TILES, BAND, H), v(2, TILES, 8, H),
            v(7, H, N), v(7, H, N), v(3, 7, 32, N), v(7, 32, N), v(3, 7, 8, N), v(7, 8, N), v(4, 7, 8, N),
            v(8, H), v(8, H), v(8, H), v(8, H), v(8, H),
            pltpu.SemaphoreType.DMA((14,)), pltpu.SemaphoreType.DMA((48,)), pltpu.SemaphoreType.DMA((48,)),
        ],
        compiler_params=pltpu.CompilerParams(
            collective_id=1, has_side_effects=True, vmem_limit_bytes=48 << 20
        ),
        cost_estimate=pl.CostEstimate(flops=10**6, bytes_accessed=40 * 10**6, transcendentals=0),
    )(canvas, obj, sums, probe, count)


STRIDE = ROWS // 8


def sweep_kernel(spot, place, canvas, obj, cl, cr, bu, bd, ol, orr, ou, od, window, probe,
                 object_new, patches_new, f0, f1, rhs, wgt, cnt, pwr, sems):
    i, j = spot[0], spot[1]
    copies = [
        pltpu.make_async_copy(canvas, rhs, sems.at[0]),
        pltpu.make_async_copy(od, f0.at[:, :, pl.ds(TILE, BAND)], sems.at[1]),
        pltpu.make_async_copy(orr, f0.at[:, pl.ds(6, 2), pl.ds(0, TILE)], sems.at[2]),
    ]
    for t in range(6):
        copies.append(pltpu.make_async_copy(
            obj.at[:, :, pl.ds(H * t, H)], f0.at[:, t, pl.ds(0, TILE)], sems.at[3 + t]))
    for c in copies:
        c.start()

    power = None
    for m in range(MODES):
        for p in range(2):
            q = probe[m, p]
            power = q * q if power is None else power + q * q
    for a in range(2):
        for b in range(2):
            pwr[a, b] = power[a * H:(a + 1) * H, b * H:(b + 1) * H].reshape(16, 8, H)
    lanes = lax.broadcasted_iota(jnp.int32, (H, TILES * H), 1)
    slot = lax.broadcasted_iota(jnp.int32, (H, TILES * H), 0)
    block = jnp.where(lanes >= 7 * H + H // 2, -1, lanes // H)
    for b in range(2):
        pick = jnp.where(slot == block - b + 2, 1.0, 0.0).astype(BF16)
        wide = dot(window[...].astype(BF16), pick)
        for r in range(10):
            line = jnp.broadcast_to(wide[r:r + 1], (8, TILES * H))
            for t in range(TILES):
                cnt[b, r, t] = line[:, t * H:(t + 1) * H]
    for c in copies:
        c.wait()

    tile = lax.broadcasted_iota(jnp.int32, (TILES, 8, H), 0)
    sub = lax.broadcasted_iota(jnp.int32, (TILES, 8, H), 1)
    lane = lax.broadcasted_iota(jnp.int32, (TILES, 8, H), 2)
    col = jnp.where(tile < 7, tile * H + lane, jnp.where(lane < H // 2, 7 * H + lane, lane - H))
    col = col + j * TILE
    col_ok = (col >= 0) & (col < 8 * TILE) & ((tile < 7) | (lane < 4) | (lane >= H - 4))
    lane1 = lax.broadcasted_iota(jnp.int32, (8, H), 1)
    sub1 = lax.broadcasted_iota(jnp.int32, (8, H), 0)

    def finish(at, den, ok, extra):
        inv = jnp.where(ok, 1.0 / (den + (0.5 + 4.0 * 16.0)), 0.0)
        wgt[:, at] = 16.0 * inv
        for p in range(2):
            field = jnp.where(ok, f0[p, :, at], 0.0)
            f0[p, :, at] = field
            rhs[p, :, at] = (rhs[p, :, at] + extra[p] + 0.5 * field) * inv

    for r in range(7):
        def step(g, carry, r=r):
            row = r * H + g * 8
            at = pl.ds(pl.multiple_of(row, 8), 8)
            den = None
            for a in range(2):
                for b in range(2):
                    term = cnt[b, r - a + 2] * pwr[a, b, g][None]
                    den = term if den is None else den + term
            ok = col_ok & (i * TILE + row < 16 * TILE)
            extra = []
            for p in range(2):
                rhs[p, 0, at] += cl[p, 1, at]
                rhs[p, 6, at] += cr[p, 0, at]
                rhs[p, 7, at] = jnp.where(lane1 < 4, cr[p, 1, at], jnp.where(lane1 >= H - 4, cl[p, 0, at], 0.0))
                if r < 6:
                    f0[p, 7, at] = jnp.where(lane1 < 4, f0[p, 7, at], ol[p, at])
                if r == 0:
                    extra.append(bu[p, :, pl.ds(pl.multiple_of(g * 8 + 8, 8), 8)])
                elif r == 6:
                    extra.append(bd[p, :, pl.ds(pl.multiple_of(g * 8, 8), 8)])
                else:
                    extra.append(0.0)
            finish(at, den, ok, extra)
            return carry

        lax.fori_loop(0, 16, step, 0)

    at = pl.ds(7 * H, 8)
    den = None
    for a in range(2):
        for b in range(2):
            low = cnt[b, 7 - a + 2] * pwr[a, b, 0][None]
            high = cnt[b, -1 - a + 2] * pwr[a, b, 15][None]
            term = jnp.where(sub < 4, low, high)
            den = term if den is None else den + term
    row_ok = ((sub < 4) & (i < 15)) | ((sub >= 4) & (i > 0))
    extra = []
    for p in range(2):
        rhs[p, :, at] = jnp.zeros((TILES, 8, H), F32)
        extra.append(jnp.where(sub < 4, bd[p, :, pl.ds(H, 8)], bu[p, :, pl.ds(0, 8)]))
        f0[p, :, at] = jnp.where(sub < 4, f0[p, :, at], ou[p])
    finish(at, den, col_ok & row_ok, extra)

    def sweep(src, dst):
        for p in range(2):
            rows = lambda t: (p, slice(None), pl.ds(t, 8, stride=STRIDE), slice(None))

            def update(t, above, here, below):
                west = jnp.concatenate([here[7:], here[:7]], axis=0)
                east = jnp.concatenate([here[1:], here[:1]], axis=0)
                west = pltpu.roll(jnp.where(lane == H - 1, west, here), 1, 2)
                east = pltpu.roll(jnp.where(lane == 0, east, here), H - 1, 2)
                near = (above + below) + (west + east)
                w = wgt[:, pl.ds(t, 8, stride=STRIDE), :]
                dst[rows(t)] = rhs[rows(t)] + w * near

            first, last = src[rows(0)], src[rows(STRIDE - 1)]

            def step(t, carry):
                above, here = carry
                below = src[rows(t + 1)]
                update(t, above, here, below)
                return here, below

            above, here = lax.fori_loop(0, STRIDE - 1, step, (pltpu.roll(last, 1, 1), first), unroll=4)
            update(STRIDE - 1, above, here, pltpu.roll(first, 7, 1))

    sweep(f0, f1)
    sweep(f1, f0)
    sweep(f0, f1)
    sweep(f1, f0)

    outs = []
    for t in range(6):
        outs.append(pltpu.make_async_copy(
            f0.at[:, t, pl.ds(0, TILE)], object_new.at[:, :, pl.ds(H * t, H)], sems.at[t]))
    for f in range(place.shape[0]):
        r = pl.multiple_of(place[f, 0], H)
        for t in range(2):
            outs.append(pltpu.make_async_copy(
                f0.at[:, place[f, 1] // H + t, pl.ds(r, N)],
                patches_new.at[f, :, :, pl.ds(H * t, H)], sems.at[6 + 2 * f + t]))
    for c in outs:
        c.start()
    for c in outs:
        c.wait()


def sweeps(spot, place, canvas, obj, cl, cr, bu, bd, ol, orr, ou, od, window, probe):
    vm, any_ = pl.BlockSpec(memory_space=pltpu.VMEM), pl.BlockSpec(memory_space=pl.ANY)
    sm = pl.BlockSpec(memory_space=pltpu.SMEM)
    v = lambda *d: pltpu.VMEM(d, F32)
    return pl.pallas_call(
        sweep_kernel,
        out_shape=[
            jax.ShapeDtypeStruct(obj.shape, F32),
            jax.ShapeDtypeStruct((place.shape[0], 2, N, N), F32),
        ],
        in_specs=[sm, sm, any_, any_, vm, vm, vm, vm, vm, any_, vm, any_, vm, vm],
        out_specs=[any_, any_],
        scratch_shapes=[
            v(2, TILES, ROWS, H), v(2, TILES, ROWS, H), v(2, TILES, ROWS, H), v(TILES, ROWS, H),
            v(2, 10, TILES, 8, H), v(2, 2, 16, 8, H), pltpu.SemaphoreType.DMA((16,)),
        ],
        compiler_params=pltpu.CompilerParams(vmem_limit_bytes=60 << 20),
    )(spot, place, canvas, obj, cl, cr, bu, bd, ol, orr, ou, od, window, probe)


def per_device(amplitude, patches, dual, probe, obj, positions):
    spot = jnp.stack([lax.axis_index("row"), lax.axis_index("col")]).astype(jnp.int32)
    place = positions - spot * TILE
    dual_new, canvas, sums, count = frames(place, amplitude, patches, dual, probe)
    cl, cr, bu, bd, ol, orr, ou, od, window, probe_new = exchange(
        canvas, obj, sums, probe.reshape(2 * MODES, N, N), count)
    object_new, patches_new = sweeps(spot, place, canvas, obj, cl, cr, bu, bd, ol, orr, ou, od, window, probe)
    return dual_new, object_new, probe_new.reshape(probe.shape), patches_new


def solution(mesh):
    return jax.shard_map(
        per_device,
        mesh=mesh,
        in_specs=(
            P(("row", "col"), None, None),
            P(("row", "col"), None, None, None),
            P(("row", "col"), None, None, None, None),
            P(),
            P(None, "row", "col"),
            P(("row", "col"), None),
        ),
        out_specs=(
            P(("row", "col"), None, None, None, None),
            P(None, "row", "col"),
            P(),
            P(("row", "col"), None, None, None),
        ),
        check_vma=False,
    )
```

```python
import math
import numpy as np
import ml_dtypes
import jax
import jax.numpy as jnp
from jax import lax
from jax.experimental import pallas as pl
from jax.experimental.pallas import tpu as pltpu
from jax.sharding import PartitionSpec as P

N = 256
H = 128
MODES = 3
TILE = 768
WIDE = TILE + H
TILES = 8
ROWS = 904
BAND = 136
LOW = TILE - 8
MESH = pl.DeviceIdType.MESH
F32, BF16 = jnp.float32, jnp.bfloat16


def dft_tables():
    k = np.arange(H)
    stacked = []
    for odd in (0, 1):
        angle = ((2 * k[:, None] + odd) * k[None, :] % N) * (2.0 * math.pi / N)
        c, s = np.cos(angle) / 16.0, np.sin(angle) / 16.0
        stacked.append(np.block([[c, s], [-s, c]]))
    whole = np.stack(stacked + [t.T for t in stacked]).astype(np.float32)
    lead = whole.astype(ml_dtypes.bfloat16)
    rest = (whole - lead.astype(np.float32)).astype(ml_dtypes.bfloat16)
    return np.stack([lead, rest], axis=1)


def order_table():
    t = np.zeros((N, N), np.float32)
    k = np.arange(H)
    t[2 * k, k] = 1.0
    t[2 * k + 1, H + k] = 1.0
    return np.stack([t, t.T]).astype(ml_dtypes.bfloat16)


def parts(x):
    lead = x.astype(BF16)
    return lead, (x - lead.astype(F32)).astype(BF16)


def dot(a, b):
    return lax.dot_general(a, b, (((1,), (0,)), ((), ())), preferred_element_type=F32)


def left(tab, which, x):
    lead, rest = parts(x)
    a, b = tab[which, 0], tab[which, 1]
    return dot(jnp.concatenate([a, a, b], axis=1), jnp.concatenate([lead, rest, lead], axis=0))


def right(tab, which, x):
    lead, rest = parts(x)
    a, b = tab[which, 0], tab[which, 1]
    return dot(jnp.concatenate([lead, rest, lead], axis=1), jnp.concatenate([a, a, b], axis=0))


def top(x):
    return x[:H]


def bot(x):
    return x[H:]


def lft(x):
    return x[:, :H]


def rgt(x):
    return x[:, H:]


def rows2(a, b):
    return jnp.concatenate([a, b], axis=0)


def cols2(a, b):
    return jnp.concatenate([a, b], axis=1)


def forward(tab, xr, xi):
    e = left(tab, 0, rows2(top(xr) + bot(xr), top(xi) + bot(xi)))
    o = left(tab, 1, rows2(top(xr) - bot(xr), top(xi) - bot(xi)))
    yr, yi = rows2(top(e), top(o)), rows2(bot(e), bot(o))
    even = right(tab, 2, cols2(lft(yr) + rgt(yr), lft(yi) + rgt(yi)))
    odd = right(tab, 3, cols2(lft(yr) - rgt(yr), lft(yi) - rgt(yi)))
    return even, odd


def inverse(tab, even, odd):
    a = right(tab, 0, even)
    b = right(tab, 1, odd)
    yr = cols2(lft(a) + lft(b), lft(a) - lft(b))
    yi = cols2(rgt(a) + rgt(b), rgt(a) - rgt(b))
    e = left(tab, 2, rows2(top(yr), top(yi)))
    o = left(tab, 3, rows2(bot(yr), bot(yi)))
    xr = rows2(top(e) + top(o), top(e) - top(o))
    xi = rows2(bot(e) + bot(o), bot(e) - bot(o))
    return xr, xi


def obj_exchange(f, obj, east, below, west, above, ends_r, ends_l, band_t, band_b, load_sem, send_sem, recv_sem):
    i, j = lax.axis_index("row"), lax.axis_index("col")
    up, down = ((i + 15) % 16, j), ((i + 1) % 16, j)
    lf, rt = (i, (j + 7) % 8), (i, (j + 1) % 8)
    first, last = pl.ds(0, BAND), pl.ds(LOW, 8)

    def remote(k, src, dst, to):
        return pltpu.make_async_remote_copy(
            src_ref=src, dst_ref=dst, send_sem=send_sem.at[k], recv_sem=recv_sem.at[k],
            device_id=to, device_id_type=MESH,
        )

    loads = []
    for t in range(6):
        lanes = pl.ds(H * t, H)
        loads.append(pltpu.make_async_copy(obj.at[:, first, lanes], band_t.at[:, t], load_sem.at[t]))
        loads.append(pltpu.make_async_copy(obj.at[:, last, lanes], band_b.at[:, t], load_sem.at[6 + t]))
    ends = []
    for n, (rows, at) in enumerate(((first, pl.ds(0, BAND)), (last, pl.ds(BAND, 8)))):
        ends.append(remote(3 * n, obj.at[:, rows, pl.ds(0, H)], ends_r.at[:, 0, at], lf))
        ends.append(remote(3 * n + 1, obj.at[:, rows, pl.ds(H, H)], ends_r.at[:, 1, at], lf))
        ends.append(remote(3 * n + 2, obj.at[:, rows, pl.ds(5 * H, H)], ends_l.at[:, at], rt))
    inner, outer = pl.ds(0, 6), pl.ds(6, 2)
    bands_in = [
        remote(6, band_t.at[:, inner], below.at[:, inner], up),
        remote(7, band_b.at[:, inner], above.at[:, inner], down),
    ]
    bands_out = [
        remote(11, band_t.at[:, outer], below.at[:, outer], up),
        remote(12, band_b.at[:, outer], above.at[:, outer], down),
    ]
    sides = [
        remote(8, obj.at[:, :, pl.ds(0, H)], east.at[:, 0], lf),
        remote(9, obj.at[:, :, pl.ds(H, H)], east.at[:, 1], lf),
        remote(10, obj.at[:, :, pl.ds(5 * H, H)], west, rt),
    ]

    @pl.when(f == 0)
    def _():
        barrier = pltpu.get_barrier_semaphore()
        for p in (up, down, lf, rt):
            pl.semaphore_signal(barrier, inc=1, device_id=p, device_id_type=MESH)
        for c in loads:
            c.start()
        pl.semaphore_wait(barrier, 4)
        for c in ends:
            c.start()
        for c in loads:
            c.wait()
        for c in bands_in + sides:
            c.start()

    @pl.when(f == 1)
    def _():
        for c in ends:
            c.wait()
        lane = lax.broadcasted_iota(jnp.int32, (1, 8, H), 2)

        def edge(g, band, to):
            src = pl.ds(pl.multiple_of(g * 8, 8), 8)
            to = pl.ds(pl.multiple_of(to * 8, 8), 8)
            band[:, 6, to] = ends_r[:, 0, src]
            band[:, 7, to] = jnp.where(
                lane < 4, ends_r[:, 1, src], jnp.where(lane >= H - 4, ends_l[:, src], 0.0))

        def step(g, carry):
            edge(g, band_t, g)
            return carry

        lax.fori_loop(0, BAND // 8, step, 0)
        edge(BAND // 8, band_b, 0)
        for c in bands_out:
            c.start()

    return bands_in + sides + bands_out


def frame_kernel(place, amp, patches, dual, probe, tab, order, obj, dual_new, parts_out, sums, count, east, below,
                 west, above, far, *shared):
    f = pl.program_id(0)
    pending = obj_exchange(f, obj, east, below, west, above, *shared)

    @pl.when(f == 0)
    def _():
        sums[...] = jnp.zeros_like(sums)
        count[...] = jnp.zeros_like(count)

    pr, pi = patches[0, 0], patches[0, 1]
    sums[6] += pr * pr + pi * pi
    power_e = power_o = None
    for m in range(MODES):
        qr, qi = probe[m, 0], probe[m, 1]
        xr = qr * pr - qi * pi + dual[0, m, 0]
        xi = qr * pi + qi * pr + dual[0, m, 1]
        even, odd = forward(tab, xr, xi)
        far[m, 0] = even
        far[m, 1] = odd
        e2 = lft(even) * lft(even) + rgt(even) * rgt(even)
        o2 = lft(odd) * lft(odd) + rgt(odd) * rgt(odd)
        power_e = e2 if power_e is None else power_e + e2
        power_o = o2 if power_o is None else power_o + o2
    lead, rest = parts(amp[0])
    a = dot(cols2(order[1], order[1]), rows2(lead, rest))
    lead, rest = parts(a)
    a = dot(cols2(lead, rest), rows2(order[0], order[0]))
    ratio_e = lft(a) * lax.rsqrt(power_e + 1.0)
    ratio_o = rgt(a) * lax.rsqrt(power_o + 1.0)
    ratio_e, ratio_o = cols2(ratio_e, ratio_e), cols2(ratio_o, ratio_o)
    obj_re = obj_im = None
    for m in range(MODES):
        qr, qi = probe[m, 0], probe[m, 1]
        nr, ni = inverse(tab, far[m, 0] * ratio_e, far[m, 1] * ratio_o)
        dr = dual[0, m, 0] + (qr * pr - qi * pi) - nr
        di = dual[0, m, 1] + (qr * pi + qi * pr) - ni
        dual_new[0, m, 0] = dr
        dual_new[0, m, 1] = di
        tr, ti = nr - dr, ni - di
        sums[2 * m] += pr * tr + pi * ti
        sums[2 * m + 1] += pr * ti - pi * tr
        re = qr * tr + qi * ti
        im = qr * ti - qi * tr
        obj_re = re if obj_re is None else obj_re + re
        obj_im = im if obj_im is None else obj_im + im
    for a in range(2):
        for b in range(2):
            for p, value in enumerate((obj_re, obj_im)):
                parts_out[0, a, b, p] = value[a * H:(a + 1) * H, b * H:(b + 1) * H]
    line = lax.broadcasted_iota(jnp.int32, (8, H), 0)
    lane = lax.broadcasted_iota(jnp.int32, (8, H), 1)
    count[...] += jnp.where((line == place[f, 0] // H) & (lane == place[f, 1] // H), 1.0, 0.0)

    @pl.when(f == pl.num_programs(0) - 1)
    def _():
        for c in pending:
            c.wait()


def frames(place, amp, patches, dual, probe, obj):
    n = amp.shape[0]
    tab, order = jnp.asarray(dft_tables()), jnp.asarray(order_table())
    whole = lambda *d: pl.BlockSpec(d, lambda f: (0,) * len(d))
    any_ = pl.BlockSpec(memory_space=pl.ANY)
    ext = pl.BlockSpec(memory_space=pl.ANY)
    f32 = lambda *d: jax.ShapeDtypeStruct(d, F32)
    v = lambda *d: pltpu.VMEM(d, F32)
    return pl.pallas_call(
        frame_kernel,
        grid=(n,),
        in_specs=[
            pl.BlockSpec(memory_space=pltpu.SMEM),
            pl.BlockSpec((1, N, N), lambda f: (f, 0, 0)),
            pl.BlockSpec((1, 2, N, N), lambda f: (f, 0, 0, 0)),
            pl.BlockSpec((1, MODES, 2, N, N), lambda f: (f, 0, 0, 0, 0)),
            whole(MODES, 2, N, N),
            whole(4, 2, N, N),
            whole(2, N, N),
            any_,
        ],
        out_specs=[
            pl.BlockSpec((1, MODES, 2, N, N), lambda f: (f, 0, 0, 0, 0)),
            pl.BlockSpec((1, 2, 2, 2, H, H), lambda f: (f, 0, 0, 0, 0, 0)),
            whole(7, N, N),
            whole(8, H),
            ext, ext, ext, ext,
        ],
        out_shape=[
            f32(*dual.shape), f32(n, 2, 2, 2, H, H), f32(7, N, N), f32(8, H),
            f32(2, 2, TILE, H), f32(2, TILES, BAND, H), f32(2, TILE, H), f32(2, TILES, 8, H),
        ],
        scratch_shapes=[
            v(MODES, 2, N, N), v(2, 2, BAND + 8, H), v(2, BAND + 8, H), v(2, TILES, BAND, H), v(2, TILES, 8, H),
            pltpu.SemaphoreType.DMA((12,)), pltpu.SemaphoreType.DMA((13,)), pltpu.SemaphoreType.DMA((13,)),
        ],
        compiler_params=pltpu.CompilerParams(
            collective_id=2, has_side_effects=True, vmem_limit_bytes=56 << 20),
    )(place, amp, patches, dual, probe, tab, order, obj)


SPAN, FIRST = 656, 120
EDGE = 280
SIDE = 56


def object_kernel(canvas_in, sums, probe, count, obj, east, below, west, above, field, probe_new,
                  canvas, cl, cr, pk_l, pk_r, in_l, in_r, bd, bu, bdh, buh, side_t, side_b, hrow_t, hrow_b,
                  f0, f1, fin, wgt, e0, e1, er, ew, wst, abv, cnt, pwr, window,
                  pair_in, half, in_1, quarter, in_2, chunk, z_all, cnt_l, cnt_r, cnt_a, cnt_u, cnt_d,
                  load_sem, send_sem, recv_sem):
    i, j = lax.axis_index("row"), lax.axis_index("col")
    y, z, x, core = i // 4, i % 4, j // 2, j % 2
    up, down = ((i + 15) % 16, j), ((i + 1) % 16, j)
    lf, rt = (i, (j + 7) % 8), (i, (j + 1) % 8)
    twin = (i, x * 2 + 1 - core)
    ys = [(((y + d) % 4) * 4 + z, j) for d in (1, 2, 3)]
    xs = [(i, ((x + d) % 4) * 2 + core) for d in (1, 2, 3)]
    zs = [(y * 4 + (z + d) % 4, j) for d in (1, 2, 3)]
    peers = [up, down, lf, rt, twin] + ys + xs + zs

    barrier = pltpu.get_barrier_semaphore()
    for p in peers:
        pl.semaphore_signal(barrier, inc=1, device_id=p, device_id_type=MESH)
    load = pltpu.make_async_copy(canvas_in, canvas.at[:, pl.ds(0, 7)], load_sem.at[0])
    load.start()
    loads = [
        pltpu.make_async_copy(below, e0.at[:, :, pl.ds(8, BAND)], load_sem.at[1]),
        pltpu.make_async_copy(below.at[:, :, pl.ds(0, 8)], f0.at[:, :, pl.ds(SPAN - 8, 8)], load_sem.at[2]),
        pltpu.make_async_copy(west, wst, load_sem.at[3]),
        pltpu.make_async_copy(above, abv, load_sem.at[4]),
    ]
    for rows, to, at in ((pl.ds(FIRST, SPAN - 8), f0, pl.ds(0, SPAN - 8)), (pl.ds(LOW, 8), e0, pl.ds(0, 8)),
                         (pl.ds(0, BAND), e0, pl.ds(ROWS - LOW, BAND))):
        for t in range(6):
            loads.append(pltpu.make_async_copy(
                obj.at[:, rows, pl.ds(H * t, H)], to.at[:, t, at], load_sem.at[1 + len(loads)]))
        loads.append(pltpu.make_async_copy(east.at[:, :, rows], to.at[:, pl.ds(6, 2), at], load_sem.at[1 + len(loads)]))
    for c in loads:
        c.start()

    used = [0]
    started = []

    def send(src, dst, to):
        k = used[0]
        used[0] += 1
        c = pltpu.make_async_remote_copy(
            src_ref=src, dst_ref=dst, send_sem=send_sem.at[k], recv_sem=recv_sem.at[k],
            device_id=to, device_id_type=MESH,
        )
        c.start()
        started.append(c)
        return c

    def landed(*copies):
        for c in copies:
            c.wait_recv()

    other = pl.ds(pl.multiple_of((1 - core) * H, H), H)
    mine = pl.ds(pl.multiple_of(core * H, H), H)

    load.wait()

    lane3 = lax.broadcasted_iota(jnp.int32, (2, SIDE, H), 2)
    pk_l[...] = jnp.zeros_like(pk_l)
    pk_r[...] = jnp.zeros_like(pk_r)

    def pack(q, carry):
        at = pl.ds(pl.multiple_of(q * SIDE, 8), SIDE)
        pk_l[...] += pltpu.roll(jnp.where(lane3 < 4, canvas[:, 1, at], 0.0), q * 8, 2)
        pk_r[...] += pltpu.roll(jnp.where(lane3 >= H - 4, canvas[:, 5, at], 0.0), q * 8, 2)
        return carry

    lax.fori_loop(0, 16, pack, 0)
    pl.semaphore_wait(barrier, len(peers))

    top_rows, low_rows, mid = pl.ds(0, BAND), pl.ds(LOW, BAND), pl.ds(BAND, LOW - BAND)
    ends = [
        send(pk_r, in_l, rt), send(pk_l, in_r, lf),
        send(count, cnt_l, rt), send(count, cnt_r, lf),
    ]
    for rows in (top_rows, low_rows):
        ends.append(send(canvas.at[:, 6, rows], cl.at[:, rows], rt))
        ends.append(send(canvas.at[:, 0, rows], cr.at[:, rows], lf))
    a_pair = send(sums.at[:, other], pair_in, twin)
    inner = pl.ds(1, 5)
    bands = [
        send(canvas.at[:, inner, pl.ds(0, H)], bd.at[:, inner], up),
        send(canvas.at[:, inner, pl.ds(TILE, H)], bu.at[:, inner], down),
    ]
    rest = [
        send(canvas.at[:, 6, mid], cl.at[:, mid], rt),
        send(canvas.at[:, 0, mid], cr.at[:, mid], lf),
    ]

    power = None
    for m in range(2 * MODES):
        q = probe[m] * probe[m]
        power = q if power is None else power + q
    for a in range(2):
        for b in range(2):
            pwr[a, b] = power[a * H:(a + 1) * H, b * H:(b + 1) * H].reshape(16, 8, H)

    landed(*ends)
    for c in ends:
        c.wait_send()
    keep = (lane3 < 4) | (lane3 >= H - 4)

    def unpack(q, carry):
        at = pl.ds(pl.multiple_of(q * SIDE, 8), SIDE)
        both = in_l[...] + in_r[...]
        canvas[:, 7, at] = jnp.where(keep, pltpu.roll(both, (H - q * 8) % H, 2), 0.0)
        return carry

    lax.fori_loop(0, 16, unpack, 0)

    def widen(first, side):
        def step(g, carry):
            at, src = pl.ds(pl.multiple_of(g * 8, 8), 8), pl.ds(pl.multiple_of(first + g * 8, 8), 8)
            side[:, 0, at] = canvas[:, 0, src] + cl[:, src]
            side[:, 1, at] = canvas[:, 6, src] + cr[:, src]
            side[:, 2, at] = canvas[:, 7, src]
            return carry

        lax.fori_loop(0, 16, step, 0)

    widen(0, side_t)
    widen(TILE, side_b)
    for row, hrow in ((H, hrow_t), (LOW, hrow_b)):
        at = pl.ds(row, 8)
        hrow[...] = canvas[:, :, at]
        hrow[:, 0] += cl[:, at]
        hrow[:, 6] += cr[:, at]
    lane2 = lax.broadcasted_iota(jnp.int32, (8, H), 1)
    cnt_a[...] = jnp.where(
        lane2 < 2, pltpu.roll(cnt_l[...], H - 4, 1),
        jnp.where(lane2 < 8, pltpu.roll(count[...], 2, 1), jnp.where(lane2 < 10, pltpu.roll(cnt_r[...], 8, 1), 0.0)),
    )
    counts = [send(cnt_a, cnt_d, up), send(cnt_a, cnt_u, down)]
    one, two = pl.ds(0, 1), pl.ds(6, 2)
    bands += [
        send(hrow_t, bdh, up), send(hrow_b, buh, down),
        send(side_t.at[:, one], bd.at[:, one], up), send(side_b.at[:, one], bu.at[:, one], down),
        send(side_t.at[:, pl.ds(1, 2)], bd.at[:, two], up), send(side_b.at[:, pl.ds(1, 2)], bu.at[:, two], down),
    ]

    landed(a_pair)
    half[...] = sums[:, mine] + pair_in[...]
    lanes = (pl.ds(0, H), pl.ds(H, H))
    path = (((y, ys), (x, xs)), ((x, xs), (y, ys)))

    def eights(at, n):
        return pl.ds(pl.multiple_of(at, 8), n)

    stage_1 = []
    for q in range(2):
        here, to = path[q][0]
        for d in (1, 2, 3):
            stage_1.append(send(half.at[:, eights(((here + d) % 4) * 32, 32), lanes[q]], in_1.at[q, d - 1], to[d - 1]))

    landed(*counts)
    line = lax.broadcasted_iota(jnp.int32, (8, H), 0)
    window[pl.ds(0, 8)] = jnp.where(line < 2, pltpu.roll(cnt_u[...], 4, 0), pltpu.roll(cnt_a[...], 2, 0))
    window[pl.ds(8, 8)] = jnp.where(line < 2, cnt_d[...], 0.0)
    wide_lane = lax.broadcasted_iota(jnp.int32, (H, TILES * H), 1)
    slot = lax.broadcasted_iota(jnp.int32, (H, TILES * H), 0)
    block_of = jnp.where(wide_lane >= 7 * H + H // 2, -1, wide_lane // H)
    for b in range(2):
        pick = jnp.where(slot == block_of - b + 2, 1.0, 0.0).astype(BF16)
        wide = dot(window[...].astype(BF16), pick)
        for r in range(10):
            row = jnp.broadcast_to(wide[r:r + 1], (8, TILES * H))
            for t in range(TILES):
                cnt[b, r, t] = row[:, t * H:(t + 1) * H]

    tile = lax.broadcasted_iota(jnp.int32, (TILES, 8, H), 0)
    sub = lax.broadcasted_iota(jnp.int32, (TILES, 8, H), 1)
    lane = lax.broadcasted_iota(jnp.int32, (TILES, 8, H), 2)
    col = jnp.where(tile < 7, tile * H + lane, jnp.where(lane < H // 2, 7 * H + lane, lane - H)) + j * TILE
    col_ok = (col >= 0) & (col < 8 * TILE) & ((tile < 7) | (lane < 4) | (lane >= H - 4))
    lane1 = lax.broadcasted_iota(jnp.int32, (8, H), 1)

    def density(r, g):
        den = None
        for a in range(2):
            for b in range(2):
                term = cnt[b, r - a + 2] * pwr[a, b, g][None]
                den = term if den is None else den + term
        return den

    def finish(src, at, to, w, ok, den, total):
        inv = jnp.where(ok, 1.0 / (den + (0.5 + 4.0 * 16.0)), 0.0)
        w[:, at] = 16.0 * inv
        for p in range(2):
            value = jnp.where(ok, src[p, :, at], 0.0)
            src[p, :, at] = value
            to[p] = (total[p] + 0.5 * value) * inv

    for c in loads:
        c.wait()
    for c in rest:
        c.wait()

    def whole_rows(p, rows):
        return jnp.concatenate(
            [canvas[p, pl.ds(0, 1), rows] + cl[p, rows][None], canvas[p, pl.ds(1, 5), rows],
             canvas[p, pl.ds(6, 1), rows] + cr[p, rows][None], canvas[p, pl.ds(7, 1), rows]], axis=0)

    def outer_tile(src, at, rows):
        for p in range(2):
            src[p, 7, at] = jnp.where(lane1 < 4, src[p, 7, at], wst[p, rows])

    for e, row in ((0, LOW), (EDGE - 8, H)):
        at = pl.ds(e, 8)
        for p in range(2):
            er[p, :, at] = whole_rows(p, pl.ds(row, 8))

    def prepare(n, carry):
        r, g = 1 + n // 16, n % 16
        row = H + n * 8
        rows, at = eights(row, 8), eights(row - FIRST, 8)
        outer_tile(f0, at, rows)
        total = [whole_rows(p, rows) for p in range(2)]

        class To:
            def __setitem__(self, p, value):
                canvas[p, :, rows] = value

        finish(f0, at, To(), wgt, col_ok, density(r, g), total)
        return carry

    lax.fori_loop(0, 80, prepare, 0)
    for at, rows in ((pl.ds(0, 8), pl.ds(H - 8, 8)), (pl.ds(SPAN - 8, 8), None)):
        wgt[:, at] = jnp.zeros((TILES, 8, H), F32)
        row_ok = (i < 15) if rows is None else (i >= 0)
        if rows is not None:
            outer_tile(f0, at, rows)
        for p in range(2):
            f0[p, :, at] = jnp.where(col_ok & row_ok, f0[p, :, at], 0.0)

    def sweep(src, a, dst, b, rhs, c, w, stride, unroll):
        rows = lambda o, t: (slice(None), slice(None), pl.ds(o + t, 8, stride=stride), slice(None))
        lane4 = lane[None]

        def update(t, over, here, under):
            left_ = jnp.concatenate([here[:, 7:], here[:, :7]], axis=1)
            right_ = jnp.concatenate([here[:, 1:], here[:, :1]], axis=1)
            left_ = pltpu.roll(jnp.where(lane4 == H - 1, left_, here), 1, 3)
            right_ = pltpu.roll(jnp.where(lane4 == 0, right_, here), H - 1, 3)
            near = (over + under) + (left_ + right_)
            dst[rows(b, t)] = rhs[rows(c, t)] + w[:, pl.ds(t, 8, stride=stride), :][None] * near

        first, last = src[rows(a, 0)], src[rows(a, stride - 1)]

        def step(t, carry):
            over, here = carry
            under = src[rows(a, t + 1)]
            update(t, over, here, under)
            return here, under

        over, here = lax.fori_loop(0, stride - 1, step, (pltpu.roll(last, 1, 2), first), unroll=unroll)
        update(stride - 1, over, here, pltpu.roll(first, 7, 2))

    landed(*stage_1)
    for q in range(2):
        here, _ = path[q][0]
        quarter[q] = half[:, eights(here * 32, 32), lanes[q]] + in_1[q, 0] + in_1[q, 1] + in_1[q, 2]
    stage_2 = []
    for q in range(2):
        here, to = path[q][1]
        for d in (1, 2, 3):
            stage_2.append(send(quarter.at[q, :, eights(((here + d) % 4) * 8, 8)], in_2.at[q, d - 1], to[d - 1]))
    sweep(f0, 0, f1, 0, canvas, FIRST, wgt, SPAN // 8, 9)
    landed(*stage_2)
    for q in range(2):
        here, _ = path[q][1]
        chunk[q] = quarter[q, :, eights(here * 8, 8)] + in_2[q, 0] + in_2[q, 1] + in_2[q, 2]
    z_all[pl.ds(z, 1)] = chunk[...][None]
    stage_3 = [send(chunk, z_all.at[z], to) for to in zs]
    sweep(f1, 0, f0, 0, canvas, FIRST, wgt, SPAN // 8, 9)
    landed(*stage_3)
    stage_4 = []
    for q in range(2):
        (outer, _), (in_, to) = path[q]
        total = z_all[0, q] + z_all[1, q] + z_all[2, q] + z_all[3, q]
        at = eights(core * H + outer * 32 + in_ * 8, 8)
        probe_new[:, at, lanes[q]] = (total[:6] + probe[:, at, lanes[q]]) / (total[6:] + 1.0)
        here = probe_new.at[:, at, lanes[q]]
        stage_4 += [send(here, here, p) for p in to]
    sweep(f0, 0, f1, 0, canvas, FIRST, wgt, SPAN // 8, 9)
    landed(*stage_4)
    stage_5 = []
    for q in range(2):
        outer, to = path[q][0]
        here = probe_new.at[:, eights(core * H + outer * 32, 32), lanes[q]]
        stage_5 += [send(here, here, p) for p in to]
    sweep(f1, 0, fin, FIRST, canvas, FIRST, wgt, SPAN // 8, 9)

    outs = []

    def copy_out(rows):
        c = pltpu.make_async_copy(fin.at[:, pl.ds(0, 7), rows], field.at[:, :, rows], load_sem.at[26 + len(outs)])
        c.start()
        outs.append(c)

    copy_out(mid)

    landed(*bands)

    def edge_step(e, r, g, rows, total, ok):
        at = pl.ds(e, 8) if isinstance(e, int) else eights(e, 8)
        if rows is not None:
            outer_tile(e0, at, rows)

        class To:
            def __setitem__(self, p, value):
                er[p, :, at] = value

        finish(e0, at, To(), ew, col_ok & ok, density(r, g), total)

    for e, row, r, g in ((0, LOW, 5, 15), (EDGE - 8, H, 1, 0)):
        edge_step(e, r, g, pl.ds(row, 8), [er[p, :, pl.ds(e, 8)] for p in range(2)], i >= 0)

    def lower(g, carry):
        rows = eights(TILE + g * 8, 8)
        at = eights(g * 8, 8)
        total = [bd[p, :, at] + whole_rows(p, rows) for p in range(2)]
        edge_step(8 + g * 8, 6, g, None, total, i < 15)
        return carry

    def upper(g, carry):
        rows = eights(g * 8, 8)
        total = [bu[p, :, rows] + whole_rows(p, rows) for p in range(2)]
        edge_step(ROWS - LOW + g * 8, 0, g, rows, total, i >= 0)
        return carry

    lax.fori_loop(0, 16, lower, 0)
    lax.fori_loop(0, 16, upper, 0)
    at = pl.ds(H + 8, 8)
    for p in range(2):
        e0[p, :, at] = jnp.where(sub < 4, e0[p, :, at], abv[p])
    total = [jnp.where(sub < 4, bdh[p], buh[p]) for p in range(2)]
    den = None
    for a in range(2):
        for b in range(2):
            low = cnt[b, 7 - a + 2] * pwr[a, b, 0][None]
            high = cnt[b, -1 - a + 2] * pwr[a, b, 15][None]
            term = jnp.where(sub < 4, low, high)
            den = term if den is None else den + term
    row_ok = ((sub < 4) & (i < 15)) | ((sub >= 4) & (i > 0))

    class To:
        def __setitem__(self, p, value):
            er[p, :, at] = value

    finish(e0, at, To(), ew, col_ok & row_ok, den, total)

    landed(*stage_5)
    here = probe_new.at[:, mine]
    stage_6 = send(here, here, twin)
    sweep(e0, 0, e1, 0, er, 0, ew, EDGE // 8, 17)
    sweep(e1, 0, e0, 0, er, 0, ew, EDGE // 8, 17)
    sweep(e0, 0, e1, 0, er, 0, ew, EDGE // 8, 17)
    sweep(e1, 0, e0, 0, er, 0, ew, EDGE // 8, 17)

    def place_edges(g, carry):
        at = eights(g * 8, 8)
        fin[:, :, at] = e0[:, :, eights(ROWS - LOW + g * 8, 8)]
        fin[:, :, eights(TILE + g * 8, 8)] = e0[:, :, eights(8 + g * 8, 8)]
        return carry

    lax.fori_loop(0, 16, place_edges, 0)
    sub4 = sub[None]
    at = pl.ds(H, 8)
    fin[:, :, at] = jnp.where(sub4 < 4, e0[:, :, pl.ds(EDGE - 8, 8)], fin[:, :, at])
    at = pl.ds(LOW, 8)
    fin[:, :, at] = jnp.where(sub4 < 4, fin[:, :, at], e0[:, :, pl.ds(0, 8)])
    copy_out(pl.ds(0, BAND))
    copy_out(pl.ds(LOW, BAND))
    landed(stage_6)
    for c in outs:
        c.wait()
    for c in started:
        if not any(c is k for k in ends + rest):
            c.wait_send()


def update_object(canvas, sums, probe, count, obj, east, below, west, above):
    f32 = lambda *d: jax.ShapeDtypeStruct(d, F32)
    vm, any_ = pl.BlockSpec(memory_space=pltpu.VMEM), pl.BlockSpec(memory_space=pl.ANY)
    v = lambda *d: pltpu.VMEM(d, F32)
    small = v(8, H)
    return pl.pallas_call(
        object_kernel,
        out_shape=[f32(2, 7, WIDE, H), f32(6, N, N)],
        in_specs=[any_, vm, vm, vm, any_, any_, any_, any_, any_],
        out_specs=[any_, vm],
        scratch_shapes=[
            v(2, TILES, WIDE, H), v(2, WIDE, H), v(2, WIDE, H),
            v(2, SIDE, H), v(2, SIDE, H), v(2, SIDE, H), v(2, SIDE, H),
            v(2, TILES, H, H), v(2, TILES, H, H), v(2, TILES, 8, H), v(2, TILES, 8, H),
            v(2, 3, H, H), v(2, 3, H, H), v(2, TILES, 8, H), v(2, TILES, 8, H),
            v(2, TILES, SPAN, H), v(2, TILES, SPAN, H), v(2, TILES, WIDE, H), v(TILES, SPAN, H),
            v(2, TILES, EDGE, H), v(2, TILES, EDGE, H), v(2, TILES, EDGE, H), v(TILES, EDGE, H),
            v(2, TILE, H), v(2, TILES, 8, H), v(2, 10, TILES, 8, H), v(2, 2, 16, 8, H), v(16, H),
            v(7, H, N), v(7, H, N), v(2, 3, 7, 32, H), v(2, 7, 32, H), v(2, 3, 7, 8, H), v(2, 7, 8, H),
            v(4, 2, 7, 8, H), small, small, small, small, small,
            pltpu.SemaphoreType.DMA((30,)), pltpu.SemaphoreType.DMA((56,)), pltpu.SemaphoreType.DMA((56,)),
        ],
        compiler_params=pltpu.CompilerParams(
            collective_id=1, has_side_effects=True, vmem_limit_bytes=62 << 20
        ),
    )(canvas, sums, probe, count, obj, east, below, west, above)


def place_kernel(place, parts_in, canvas):
    canvas[...] = jnp.zeros_like(canvas)
    for f in range(parts_in.shape[0]):
        r, c = pl.multiple_of(place[f, 0], H), place[f, 1] // H
        for a in range(2):
            for b in range(2):
                for p in range(2):
                    canvas[p, c + b, pl.ds(r + a * H, H)] += parts_in[f, a, b, p]


def place_frames(place, con):
    vm = pl.BlockSpec(memory_space=pltpu.VMEM)
    return pl.pallas_call(
        place_kernel,
        out_shape=jax.ShapeDtypeStruct((2, 7, WIDE, H), F32),
        in_specs=[pl.BlockSpec(memory_space=pltpu.SMEM), vm],
        out_specs=vm,
        compiler_params=pltpu.CompilerParams(vmem_limit_bytes=40 << 20),
    )(place, con)


def window_kernel(place, field, object_new, patches_new, sems):
    outs = []
    for t in range(6):
        outs.append(pltpu.make_async_copy(
            field.at[:, t, pl.ds(0, TILE)], object_new.at[:, :, pl.ds(H * t, H)], sems.at[t]))
    for f in range(place.shape[0]):
        r, c = pl.multiple_of(place[f, 0], H), place[f, 1] // H
        for t in range(2):
            outs.append(pltpu.make_async_copy(
                field.at[:, c + t, pl.ds(r, N)], patches_new.at[f, :, :, pl.ds(H * t, H)], sems.at[6 + 2 * f + t]))
    for c in outs:
        c.start()
    for c in outs:
        c.wait()


def windows(place, field):
    vm, any_ = pl.BlockSpec(memory_space=pltpu.VMEM), pl.BlockSpec(memory_space=pl.ANY)
    f32 = lambda *d: jax.ShapeDtypeStruct(d, F32)
    n = place.shape[0]
    return pl.pallas_call(
        window_kernel,
        out_shape=[f32(2, TILE, TILE), f32(n, 2, N, N)],
        in_specs=[pl.BlockSpec(memory_space=pltpu.SMEM), vm],
        out_specs=[any_, any_],
        scratch_shapes=[pltpu.SemaphoreType.DMA((6 + 2 * n,))],
        compiler_params=pltpu.CompilerParams(vmem_limit_bytes=40 << 20),
    )(place, field)


def per_device(amplitude, patches, dual, probe, obj, positions):
    spot = jnp.stack([lax.axis_index("row"), lax.axis_index("col")]).astype(jnp.int32)
    place = positions - spot * TILE
    dual_new, con, sums, count, *around = frames(place, amplitude, patches, dual, probe, obj)
    canvas = place_frames(place, con)
    field, probe_new = update_object(canvas, sums, probe.reshape(2 * MODES, N, N), count, obj, *around)
    object_new, patches_new = windows(place, field)
    return dual_new, object_new, probe_new.reshape(probe.shape), patches_new


def solution(mesh):
    return jax.shard_map(
        per_device,
        mesh=mesh,
        in_specs=(
            P(("row", "col"), None, None),
            P(("row", "col"), None, None, None),
            P(("row", "col"), None, None, None, None),
            P(),
            P(None, "row", "col"),
            P(("row", "col"), None),
        ),
        out_specs=(
            P(("row", "col"), None, None, None, None),
            P(None, "row", "col"),
            P(),
            P(("row", "col"), None, None, None),
        ),
        check_vma=False,
    )
```

```python
import math
import numpy as np
import ml_dtypes
import jax
import jax.numpy as jnp
from jax import lax
from jax.experimental import pallas as pl
from jax.experimental.pallas import tpu as pltpu
from jax.sharding import PartitionSpec as P

N = 256
H = 128
MODES = 3
TILE = 768
WIDE = TILE + H
TILES = 8
ROWS = 904
BAND = 136
LOW = TILE - 8
MESH = pl.DeviceIdType.MESH
F32, BF16 = jnp.float32, jnp.bfloat16


def dft_tables():
    k = np.arange(H)
    stacked = []
    for odd in (0, 1):
        angle = ((2 * k[:, None] + odd) * k[None, :] % N) * (2.0 * math.pi / N)
        c, s = np.cos(angle) / 16.0, np.sin(angle) / 16.0
        stacked.append(np.block([[c, s], [-s, c]]))
    whole = np.stack(stacked + [t.T for t in stacked]).astype(np.float32)
    lead = whole.astype(ml_dtypes.bfloat16)
    rest = (whole - lead.astype(np.float32)).astype(ml_dtypes.bfloat16)
    return np.stack([lead, rest], axis=1)


def order_table():
    t = np.zeros((N, N), np.float32)
    k = np.arange(H)
    t[2 * k, k] = 1.0
    t[2 * k + 1, H + k] = 1.0
    return np.stack([t, t.T]).astype(ml_dtypes.bfloat16)


def parts(x):
    lead = x.astype(BF16)
    return lead, (x - lead.astype(F32)).astype(BF16)


def dot(a, b):
    return lax.dot_general(a, b, (((1,), (0,)), ((), ())), preferred_element_type=F32)


def left(tab, which, x):
    lead, rest = parts(x)
    a, b = tab[which, 0], tab[which, 1]
    return dot(jnp.concatenate([a, a, b], axis=1), jnp.concatenate([lead, rest, lead], axis=0))


def right(tab, which, x):
    lead, rest = parts(x)
    a, b = tab[which, 0], tab[which, 1]
    return dot(jnp.concatenate([lead, rest, lead], axis=1), jnp.concatenate([a, a, b], axis=0))


def top(x):
    return x[:H]


def bot(x):
    return x[H:]


def lft(x):
    return x[:, :H]


def rgt(x):
    return x[:, H:]


def rows2(a, b):
    return jnp.concatenate([a, b], axis=0)


def cols2(a, b):
    return jnp.concatenate([a, b], axis=1)


def forward(tab, xr, xi):
    e = left(tab, 0, rows2(top(xr) + bot(xr), top(xi) + bot(xi)))
    o = left(tab, 1, rows2(top(xr) - bot(xr), top(xi) - bot(xi)))
    yr, yi = rows2(top(e), top(o)), rows2(bot(e), bot(o))
    even = right(tab, 2, cols2(lft(yr) + rgt(yr), lft(yi) + rgt(yi)))
    odd = right(tab, 3, cols2(lft(yr) - rgt(yr), lft(yi) - rgt(yi)))
    return even, odd


def inverse(tab, even, odd):
    a = right(tab, 0, even)
    b = right(tab, 1, odd)
    yr = cols2(lft(a) + lft(b), lft(a) - lft(b))
    yi = cols2(rgt(a) + rgt(b), rgt(a) - rgt(b))
    e = left(tab, 2, rows2(top(yr), top(yi)))
    o = left(tab, 3, rows2(bot(yr), bot(yi)))
    xr = rows2(top(e) + top(o), top(e) - top(o))
    xi = rows2(bot(e) + bot(o), bot(e) - bot(o))
    return xr, xi


def obj_exchange(f, obj, east, below, west, above, ends_r, ends_l, band_t, band_b, load_sem, send_sem, recv_sem):
    i, j = lax.axis_index("row"), lax.axis_index("col")
    up, down = ((i + 15) % 16, j), ((i + 1) % 16, j)
    lf, rt = (i, (j + 7) % 8), (i, (j + 1) % 8)
    first, last = pl.ds(0, BAND), pl.ds(LOW, 8)

    def remote(k, src, dst, to):
        return pltpu.make_async_remote_copy(
            src_ref=src, dst_ref=dst, send_sem=send_sem.at[k], recv_sem=recv_sem.at[k],
            device_id=to, device_id_type=MESH,
        )

    loads = []
    for t in range(6):
        lanes = pl.ds(H * t, H)
        loads.append(pltpu.make_async_copy(obj.at[:, first, lanes], band_t.at[:, t], load_sem.at[t]))
        loads.append(pltpu.make_async_copy(obj.at[:, last, lanes], band_b.at[:, t], load_sem.at[6 + t]))
    ends = []
    for n, (rows, at) in enumerate(((first, pl.ds(0, BAND)), (last, pl.ds(BAND, 8)))):
        ends.append(remote(3 * n, obj.at[:, rows, pl.ds(0, H)], ends_r.at[:, 0, at], lf))
        ends.append(remote(3 * n + 1, obj.at[:, rows, pl.ds(H, H)], ends_r.at[:, 1, at], lf))
        ends.append(remote(3 * n + 2, obj.at[:, rows, pl.ds(5 * H, H)], ends_l.at[:, at], rt))
    inner, outer = pl.ds(0, 6), pl.ds(6, 2)
    bands_in = [
        remote(6, band_t.at[:, inner], below.at[:, inner], up),
        remote(7, band_b.at[:, inner], above.at[:, inner], down),
    ]
    bands_out = [
        remote(11, band_t.at[:, outer], below.at[:, outer], up),
        remote(12, band_b.at[:, outer], above.at[:, outer], down),
    ]
    sides = [
        remote(8, obj.at[:, :, pl.ds(0, H)], east.at[:, 0], lf),
        remote(9, obj.at[:, :, pl.ds(H, H)], east.at[:, 1], lf),
        remote(10, obj.at[:, :, pl.ds(5 * H, H)], west, rt),
    ]

    @pl.when(f == 0)
    def _():
        barrier = pltpu.get_barrier_semaphore()
        for p in (up, down, lf, rt):
            pl.semaphore_signal(barrier, inc=1, device_id=p, device_id_type=MESH)
        for c in loads:
            c.start()
        pl.semaphore_wait(barrier, 4)
        for c in ends:
            c.start()
        for c in loads:
            c.wait()
        for c in bands_in + sides:
            c.start()

    @pl.when(f == 1)
    def _():
        for c in ends:
            c.wait()
        lane = lax.broadcasted_iota(jnp.int32, (1, 8, H), 2)

        def edge(g, band, to):
            src = pl.ds(pl.multiple_of(g * 8, 8), 8)
            to = pl.ds(pl.multiple_of(to * 8, 8), 8)
            band[:, 6, to] = ends_r[:, 0, src]
            band[:, 7, to] = jnp.where(
                lane < 4, ends_r[:, 1, src], jnp.where(lane >= H - 4, ends_l[:, src], 0.0))

        def step(g, carry):
            edge(g, band_t, g)
            return carry

        lax.fori_loop(0, BAND // 8, step, 0)
        edge(BAND // 8, band_b, 0)
        for c in bands_out:
            c.start()

    return bands_in + sides + bands_out


def frame_kernel(place, amp, patches, dual, probe, tab, order, obj, dual_new, parts_out, sums, count, east, below,
                 west, above, far, *shared):
    f = pl.program_id(0)
    pending = obj_exchange(f, obj, east, below, west, above, *shared)

    @pl.when(f == 0)
    def _():
        sums[...] = jnp.zeros_like(sums)
        count[...] = jnp.zeros_like(count)

    pr, pi = patches[0, 0], patches[0, 1]
    sums[6] += pr * pr + pi * pi
    power_e = power_o = None
    for m in range(MODES):
        qr, qi = probe[m, 0], probe[m, 1]
        xr = qr * pr - qi * pi + dual[0, m, 0]
        xi = qr * pi + qi * pr + dual[0, m, 1]
        even, odd = forward(tab, xr, xi)
        far[m, 0] = even
        far[m, 1] = odd
        e2 = lft(even) * lft(even) + rgt(even) * rgt(even)
        o2 = lft(odd) * lft(odd) + rgt(odd) * rgt(odd)
        power_e = e2 if power_e is None else power_e + e2
        power_o = o2 if power_o is None else power_o + o2
    lead, rest = parts(amp[0])
    a = dot(cols2(order[1], order[1]), rows2(lead, rest))
    lead, rest = parts(a)
    a = dot(cols2(lead, rest), rows2(order[0], order[0]))
    ratio_e = lft(a) * lax.rsqrt(power_e + 1.0)
    ratio_o = rgt(a) * lax.rsqrt(power_o + 1.0)
    ratio_e, ratio_o = cols2(ratio_e, ratio_e), cols2(ratio_o, ratio_o)
    obj_re = obj_im = None
    for m in range(MODES):
        qr, qi = probe[m, 0], probe[m, 1]
        nr, ni = inverse(tab, far[m, 0] * ratio_e, far[m, 1] * ratio_o)
        dr = dual[0, m, 0] + (qr * pr - qi * pi) - nr
        di = dual[0, m, 1] + (qr * pi + qi * pr) - ni
        dual_new[0, m, 0] = dr
        dual_new[0, m, 1] = di
        tr, ti = nr - dr, ni - di
        sums[2 * m] += pr * tr + pi * ti
        sums[2 * m + 1] += pr * ti - pi * tr
        re = qr * tr + qi * ti
        im = qr * ti - qi * tr
        obj_re = re if obj_re is None else obj_re + re
        obj_im = im if obj_im is None else obj_im + im
    for a in range(2):
        for b in range(2):
            for p, value in enumerate((obj_re, obj_im)):
                parts_out[0, a, b, p] = value[a * H:(a + 1) * H, b * H:(b + 1) * H]
    line = lax.broadcasted_iota(jnp.int32, (8, H), 0)
    lane = lax.broadcasted_iota(jnp.int32, (8, H), 1)
    count[...] += jnp.where((line == place[f, 0] // H) & (lane == place[f, 1] // H), 1.0, 0.0)

    @pl.when(f == pl.num_programs(0) - 1)
    def _():
        for c in pending:
            c.wait()


def frames(place, amp, patches, dual, probe, obj):
    n = amp.shape[0]
    tab, order = jnp.asarray(dft_tables()), jnp.asarray(order_table())
    whole = lambda *d: pl.BlockSpec(d, lambda f: (0,) * len(d))
    any_ = pl.BlockSpec(memory_space=pl.ANY)
    ext = pl.BlockSpec(memory_space=pl.ANY)
    f32 = lambda *d: jax.ShapeDtypeStruct(d, F32)
    v = lambda *d: pltpu.VMEM(d, F32)
    return pl.pallas_call(
        frame_kernel,
        grid=(n,),
        in_specs=[
            pl.BlockSpec(memory_space=pltpu.SMEM),
            pl.BlockSpec((1, N, N), lambda f: (f, 0, 0)),
            pl.BlockSpec((1, 2, N, N), lambda f: (f, 0, 0, 0)),
            pl.BlockSpec((1, MODES, 2, N, N), lambda f: (f, 0, 0, 0, 0)),
            whole(MODES, 2, N, N),
            whole(4, 2, N, N),
            whole(2, N, N),
            any_,
        ],
        out_specs=[
            pl.BlockSpec((1, MODES, 2, N, N), lambda f: (f, 0, 0, 0, 0)),
            pl.BlockSpec((1, 2, 2, 2, H, H), lambda f: (f, 0, 0, 0, 0, 0)),
            whole(7, N, N),
            whole(8, H),
            ext, ext, ext, ext,
        ],
        out_shape=[
            f32(*dual.shape), f32(n, 2, 2, 2, H, H), f32(7, N, N), f32(8, H),
            f32(2, 2, TILE, H), f32(2, TILES, BAND, H), f32(2, TILE, H), f32(2, TILES, 8, H),
        ],
        scratch_shapes=[
            v(MODES, 2, N, N), v(2, 2, BAND + 8, H), v(2, BAND + 8, H), v(2, TILES, BAND, H), v(2, TILES, 8, H),
            pltpu.SemaphoreType.DMA((12,)), pltpu.SemaphoreType.DMA((13,)), pltpu.SemaphoreType.DMA((13,)),
        ],
        compiler_params=pltpu.CompilerParams(
            collective_id=2, has_side_effects=True, vmem_limit_bytes=56 << 20),
    )(place, amp, patches, dual, probe, tab, order, obj)


SPAN, FIRST = 656, 120
EDGE = 280
SIDE = 56


def object_kernel(canvas_in, sums, probe, count, obj, east, below, west, above, field, probe_new,
                  canvas, cl, cr, pk_l, pk_r, in_l, in_r, bd, bu, bdh, buh, side_t, side_b, hrow_t, hrow_b,
                  f0, f1, fin, wgt, e0, e1, er, ew, wst, abv, cnt, pwr, window,
                  pair_in, half, in_1, quarter, in_2, chunk, z_all, cnt_l, cnt_r, cnt_a, cnt_u, cnt_d,
                  load_sem, send_sem, recv_sem):
    i, j = lax.axis_index("row"), lax.axis_index("col")
    y, z, x, core = i // 4, i % 4, j // 2, j % 2
    up, down = ((i + 15) % 16, j), ((i + 1) % 16, j)
    lf, rt = (i, (j + 7) % 8), (i, (j + 1) % 8)
    twin = (i, x * 2 + 1 - core)
    ys = [(((y + d) % 4) * 4 + z, j) for d in (1, 2, 3)]
    xs = [(i, ((x + d) % 4) * 2 + core) for d in (1, 2, 3)]
    zs = [(y * 4 + (z + d) % 4, j) for d in (1, 2, 3)]
    peers = [up, down, lf, rt, twin] + ys + xs + zs

    barrier = pltpu.get_barrier_semaphore()
    for p in peers:
        pl.semaphore_signal(barrier, inc=1, device_id=p, device_id_type=MESH)
    load = pltpu.make_async_copy(canvas_in, canvas.at[:, pl.ds(0, 7)], load_sem.at[0])
    load.start()
    loads = [
        pltpu.make_async_copy(below, e0.at[:, :, pl.ds(8, BAND)], load_sem.at[1]),
        pltpu.make_async_copy(below.at[:, :, pl.ds(0, 8)], f0.at[:, :, pl.ds(SPAN - 8, 8)], load_sem.at[2]),
        pltpu.make_async_copy(west, wst, load_sem.at[3]),
        pltpu.make_async_copy(above, abv, load_sem.at[4]),
    ]
    for rows, to, at in ((pl.ds(FIRST, SPAN - 8), f0, pl.ds(0, SPAN - 8)), (pl.ds(LOW, 8), e0, pl.ds(0, 8)),
                         (pl.ds(0, BAND), e0, pl.ds(ROWS - LOW, BAND))):
        for t in range(6):
            loads.append(pltpu.make_async_copy(
                obj.at[:, rows, pl.ds(H * t, H)], to.at[:, t, at], load_sem.at[1 + len(loads)]))
        loads.append(pltpu.make_async_copy(east.at[:, :, rows], to.at[:, pl.ds(6, 2), at], load_sem.at[1 + len(loads)]))
    for c in loads:
        c.start()

    used = [0]
    started = []

    def send(src, dst, to):
        k = used[0]
        used[0] += 1
        c = pltpu.make_async_remote_copy(
            src_ref=src, dst_ref=dst, send_sem=send_sem.at[k], recv_sem=recv_sem.at[k],
            device_id=to, device_id_type=MESH,
        )
        c.start()
        started.append(c)
        return c

    def landed(*copies):
        for c in copies:
            c.wait_recv()

    other = pl.ds(pl.multiple_of((1 - core) * H, H), H)
    mine = pl.ds(pl.multiple_of(core * H, H), H)

    load.wait()

    lane3 = lax.broadcasted_iota(jnp.int32, (2, SIDE, H), 2)
    pk_l[...] = jnp.zeros_like(pk_l)
    pk_r[...] = jnp.zeros_like(pk_r)

    def pack(q, carry):
        at = pl.ds(pl.multiple_of(q * SIDE, 8), SIDE)
        pk_l[...] += pltpu.roll(jnp.where(lane3 < 4, canvas[:, 1, at], 0.0), q * 8, 2)
        pk_r[...] += pltpu.roll(jnp.where(lane3 >= H - 4, canvas[:, 5, at], 0.0), q * 8, 2)
        return carry

    lax.fori_loop(0, 16, pack, 0)
    pl.semaphore_wait(barrier, len(peers))

    top_rows, low_rows, mid = pl.ds(0, BAND), pl.ds(LOW, BAND), pl.ds(BAND, LOW - BAND)
    a_pair = send(sums.at[:, other], pair_in, twin)
    ends = [
        send(pk_r, in_l, rt), send(pk_l, in_r, lf),
        send(count, cnt_l, rt), send(count, cnt_r, lf),
    ]
    for rows in (top_rows, low_rows):
        ends.append(send(canvas.at[:, 6, rows], cl.at[:, rows], rt))
        ends.append(send(canvas.at[:, 0, rows], cr.at[:, rows], lf))
    inner = pl.ds(1, 5)
    bands = [
        send(canvas.at[:, inner, pl.ds(0, H)], bd.at[:, inner], up),
        send(canvas.at[:, inner, pl.ds(TILE, H)], bu.at[:, inner], down),
    ]
    rest = [
        send(canvas.at[:, 6, mid], cl.at[:, mid], rt),
        send(canvas.at[:, 0, mid], cr.at[:, mid], lf),
    ]

    power = None
    for m in range(2 * MODES):
        q = probe[m] * probe[m]
        power = q if power is None else power + q
    for a in range(2):
        for b in range(2):
            pwr[a, b] = power[a * H:(a + 1) * H, b * H:(b + 1) * H].reshape(16, 8, H)

    landed(a_pair)
    half[...] = sums[:, mine] + pair_in[...]
    lanes = (pl.ds(0, H), pl.ds(H, H))
    path = (((y, ys), (x, xs)), ((x, xs), (y, ys)))

    def eights(at, n):
        return pl.ds(pl.multiple_of(at, 8), n)

    stage_1 = []
    for q in range(2):
        here, to = path[q][0]
        for d in (1, 2, 3):
            stage_1.append(send(half.at[:, eights(((here + d) % 4) * 32, 32), lanes[q]], in_1.at[q, d - 1], to[d - 1]))

    landed(*ends)
    for c in ends:
        c.wait_send()
    keep = (lane3 < 4) | (lane3 >= H - 4)

    def unpack(q, carry):
        at = pl.ds(pl.multiple_of(q * SIDE, 8), SIDE)
        both = in_l[...] + in_r[...]
        canvas[:, 7, at] = jnp.where(keep, pltpu.roll(both, (H - q * 8) % H, 2), 0.0)
        return carry

    lax.fori_loop(0, 16, unpack, 0)

    def widen(first, side):
        def step(g, carry):
            at, src = pl.ds(pl.multiple_of(g * 8, 8), 8), pl.ds(pl.multiple_of(first + g * 8, 8), 8)
            side[:, 0, at] = canvas[:, 0, src] + cl[:, src]
            side[:, 1, at] = canvas[:, 6, src] + cr[:, src]
            side[:, 2, at] = canvas[:, 7, src]
            return carry

        lax.fori_loop(0, 16, step, 0)

    widen(0, side_t)
    widen(TILE, side_b)
    for row, hrow in ((H, hrow_t), (LOW, hrow_b)):
        at = pl.ds(row, 8)
        hrow[...] = canvas[:, :, at]
        hrow[:, 0] += cl[:, at]
        hrow[:, 6] += cr[:, at]
    lane2 = lax.broadcasted_iota(jnp.int32, (8, H), 1)
    cnt_a[...] = jnp.where(
        lane2 < 2, pltpu.roll(cnt_l[...], H - 4, 1),
        jnp.where(lane2 < 8, pltpu.roll(count[...], 2, 1), jnp.where(lane2 < 10, pltpu.roll(cnt_r[...], 8, 1), 0.0)),
    )
    counts = [send(cnt_a, cnt_d, up), send(cnt_a, cnt_u, down)]
    one, two = pl.ds(0, 1), pl.ds(6, 2)
    bands += [
        send(hrow_t, bdh, up), send(hrow_b, buh, down),
        send(side_t.at[:, one], bd.at[:, one], up), send(side_b.at[:, one], bu.at[:, one], down),
        send(side_t.at[:, pl.ds(1, 2)], bd.at[:, two], up), send(side_b.at[:, pl.ds(1, 2)], bu.at[:, two], down),
    ]

    landed(*counts)
    line = lax.broadcasted_iota(jnp.int32, (8, H), 0)
    window[pl.ds(0, 8)] = jnp.where(line < 2, pltpu.roll(cnt_u[...], 4, 0), pltpu.roll(cnt_a[...], 2, 0))
    window[pl.ds(8, 8)] = jnp.where(line < 2, cnt_d[...], 0.0)
    wide_lane = lax.broadcasted_iota(jnp.int32, (H, TILES * H), 1)
    slot = lax.broadcasted_iota(jnp.int32, (H, TILES * H), 0)
    block_of = jnp.where(wide_lane >= 7 * H + H // 2, -1, wide_lane // H)
    for b in range(2):
        pick = jnp.where(slot == block_of - b + 2, 1.0, 0.0).astype(BF16)
        wide = dot(window[...].astype(BF16), pick)
        for r in range(10):
            row = jnp.broadcast_to(wide[r:r + 1], (8, TILES * H))
            for t in range(TILES):
                cnt[b, r, t] = row[:, t * H:(t + 1) * H]

    tile = lax.broadcasted_iota(jnp.int32, (TILES, 8, H), 0)
    sub = lax.broadcasted_iota(jnp.int32, (TILES, 8, H), 1)
    lane = lax.broadcasted_iota(jnp.int32, (TILES, 8, H), 2)
    col = jnp.where(tile < 7, tile * H + lane, jnp.where(lane < H // 2, 7 * H + lane, lane - H)) + j * TILE
    col_ok = (col >= 0) & (col < 8 * TILE) & ((tile < 7) | (lane < 4) | (lane >= H - 4))
    lane1 = lax.broadcasted_iota(jnp.int32, (8, H), 1)

    def density(r, g):
        den = None
        for a in range(2):
            for b in range(2):
                term = cnt[b, r - a + 2] * pwr[a, b, g][None]
                den = term if den is None else den + term
        return den

    def finish(src, at, to, w, ok, den, total):
        inv = jnp.where(ok, 1.0 / (den + (0.5 + 4.0 * 16.0)), 0.0)
        w[:, at] = 16.0 * inv
        for p in range(2):
            value = jnp.where(ok, src[p, :, at], 0.0)
            src[p, :, at] = value
            to[p] = (total[p] + 0.5 * value) * inv

    for c in loads:
        c.wait()
    for c in rest:
        c.wait()

    def whole_rows(p, rows):
        return jnp.concatenate(
            [canvas[p, pl.ds(0, 1), rows] + cl[p, rows][None], canvas[p, pl.ds(1, 5), rows],
             canvas[p, pl.ds(6, 1), rows] + cr[p, rows][None], canvas[p, pl.ds(7, 1), rows]], axis=0)

    def outer_tile(src, at, rows):
        for p in range(2):
            src[p, 7, at] = jnp.where(lane1 < 4, src[p, 7, at], wst[p, rows])

    for e, row in ((0, LOW), (EDGE - 8, H)):
        at = pl.ds(e, 8)
        for p in range(2):
            er[p, :, at] = whole_rows(p, pl.ds(row, 8))

    def prepare(n, carry):
        r, g = 1 + n // 16, n % 16
        row = H + n * 8
        rows, at = eights(row, 8), eights(row - FIRST, 8)
        outer_tile(f0, at, rows)
        total = [whole_rows(p, rows) for p in range(2)]

        class To:
            def __setitem__(self, p, value):
                canvas[p, :, rows] = value

        finish(f0, at, To(), wgt, col_ok, density(r, g), total)
        return carry

    lax.fori_loop(0, 80, prepare, 0)
    for at, rows in ((pl.ds(0, 8), pl.ds(H - 8, 8)), (pl.ds(SPAN - 8, 8), None)):
        wgt[:, at] = jnp.zeros((TILES, 8, H), F32)
        row_ok = (i < 15) if rows is None else (i >= 0)
        if rows is not None:
            outer_tile(f0, at, rows)
        for p in range(2):
            f0[p, :, at] = jnp.where(col_ok & row_ok, f0[p, :, at], 0.0)

    def sweep(src, a, dst, b, rhs, c, w, stride, unroll):
        rows = lambda o, t: (slice(None), slice(None), pl.ds(o + t, 8, stride=stride), slice(None))
        lane4 = lane[None]

        def update(t, over, here, under):
            left_ = jnp.concatenate([here[:, 7:], here[:, :7]], axis=1)
            right_ = jnp.concatenate([here[:, 1:], here[:, :1]], axis=1)
            left_ = pltpu.roll(jnp.where(lane4 == H - 1, left_, here), 1, 3)
            right_ = pltpu.roll(jnp.where(lane4 == 0, right_, here), H - 1, 3)
            near = (over + under) + (left_ + right_)
            dst[rows(b, t)] = rhs[rows(c, t)] + w[:, pl.ds(t, 8, stride=stride), :][None] * near

        first, last = src[rows(a, 0)], src[rows(a, stride - 1)]

        def step(t, carry):
            over, here = carry
            under = src[rows(a, t + 1)]
            update(t, over, here, under)
            return here, under

        over, here = lax.fori_loop(0, stride - 1, step, (pltpu.roll(last, 1, 2), first), unroll=unroll)
        update(stride - 1, over, here, pltpu.roll(first, 7, 2))

    landed(*stage_1)
    for q in range(2):
        here, _ = path[q][0]
        quarter[q] = half[:, eights(here * 32, 32), lanes[q]] + in_1[q, 0] + in_1[q, 1] + in_1[q, 2]
    stage_2 = []
    for q in range(2):
        here, to = path[q][1]
        for d in (1, 2, 3):
            stage_2.append(send(quarter.at[q, :, eights(((here + d) % 4) * 8, 8)], in_2.at[q, d - 1], to[d - 1]))
    sweep(f0, 0, f1, 0, canvas, FIRST, wgt, SPAN // 8, 9)
    landed(*stage_2)
    for q in range(2):
        here, _ = path[q][1]
        chunk[q] = quarter[q, :, eights(here * 8, 8)] + in_2[q, 0] + in_2[q, 1] + in_2[q, 2]
    z_all[pl.ds(z, 1)] = chunk[...][None]
    stage_3 = [send(chunk, z_all.at[z], to) for to in zs]
    sweep(f1, 0, f0, 0, canvas, FIRST, wgt, SPAN // 8, 9)
    landed(*stage_3)
    stage_4 = []
    for q in range(2):
        (outer, _), (in_, to) = path[q]
        total = z_all[0, q] + z_all[1, q] + z_all[2, q] + z_all[3, q]
        at = eights(core * H + outer * 32 + in_ * 8, 8)
        probe_new[:, at, lanes[q]] = (total[:6] + probe[:, at, lanes[q]]) / (total[6:] + 1.0)
        here = probe_new.at[:, at, lanes[q]]
        stage_4 += [send(here, here, p) for p in to]
    sweep(f0, 0, f1, 0, canvas, FIRST, wgt, SPAN // 8, 9)
    landed(*stage_4)
    stage_5 = []
    for q in range(2):
        outer, to = path[q][0]
        here = probe_new.at[:, eights(core * H + outer * 32, 32), lanes[q]]
        stage_5 += [send(here, here, p) for p in to]
    sweep(f1, 0, fin, FIRST, canvas, FIRST, wgt, SPAN // 8, 9)

    outs = []

    def copy_out(rows):
        c = pltpu.make_async_copy(fin.at[:, pl.ds(0, 7), rows], field.at[:, :, rows], load_sem.at[26 + len(outs)])
        c.start()
        outs.append(c)

    copy_out(mid)

    landed(*bands)

    def edge_step(e, r, g, rows, total, ok):
        at = pl.ds(e, 8) if isinstance(e, int) else eights(e, 8)
        if rows is not None:
            outer_tile(e0, at, rows)

        class To:
            def __setitem__(self, p, value):
                er[p, :, at] = value

        finish(e0, at, To(), ew, col_ok & ok, density(r, g), total)

    for e, row, r, g in ((0, LOW, 5, 15), (EDGE - 8, H, 1, 0)):
        edge_step(e, r, g, pl.ds(row, 8), [er[p, :, pl.ds(e, 8)] for p in range(2)], i >= 0)

    def lower(g, carry):
        rows = eights(TILE + g * 8, 8)
        at = eights(g * 8, 8)
        total = [bd[p, :, at] + whole_rows(p, rows) for p in range(2)]
        edge_step(8 + g * 8, 6, g, None, total, i < 15)
        return carry

    def upper(g, carry):
        rows = eights(g * 8, 8)
        total = [bu[p, :, rows] + whole_rows(p, rows) for p in range(2)]
        edge_step(ROWS - LOW + g * 8, 0, g, rows, total, i >= 0)
        return carry

    lax.fori_loop(0, 16, lower, 0)
    lax.fori_loop(0, 16, upper, 0)
    at = pl.ds(H + 8, 8)
    for p in range(2):
        e0[p, :, at] = jnp.where(sub < 4, e0[p, :, at], abv[p])
    total = [jnp.where(sub < 4, bdh[p], buh[p]) for p in range(2)]
    den = None
    for a in range(2):
        for b in range(2):
            low = cnt[b, 7 - a + 2] * pwr[a, b, 0][None]
            high = cnt[b, -1 - a + 2] * pwr[a, b, 15][None]
            term = jnp.where(sub < 4, low, high)
            den = term if den is None else den + term
    row_ok = ((sub < 4) & (i < 15)) | ((sub >= 4) & (i > 0))

    class To:
        def __setitem__(self, p, value):
            er[p, :, at] = value

    finish(e0, at, To(), ew, col_ok & row_ok, den, total)

    landed(*stage_5)
    here = probe_new.at[:, mine]
    stage_6 = send(here, here, twin)
    sweep(e0, 0, e1, 0, er, 0, ew, EDGE // 8, 17)
    sweep(e1, 0, e0, 0, er, 0, ew, EDGE // 8, 17)
    sweep(e0, 0, e1, 0, er, 0, ew, EDGE // 8, 17)
    sweep(e1, 0, e0, 0, er, 0, ew, EDGE // 8, 17)

    def place_edges(g, carry):
        at = eights(g * 8, 8)
        fin[:, :, at] = e0[:, :, eights(ROWS - LOW + g * 8, 8)]
        fin[:, :, eights(TILE + g * 8, 8)] = e0[:, :, eights(8 + g * 8, 8)]
        return carry

    lax.fori_loop(0, 16, place_edges, 0)
    sub4 = sub[None]
    at = pl.ds(H, 8)
    fin[:, :, at] = jnp.where(sub4 < 4, e0[:, :, pl.ds(EDGE - 8, 8)], fin[:, :, at])
    at = pl.ds(LOW, 8)
    fin[:, :, at] = jnp.where(sub4 < 4, fin[:, :, at], e0[:, :, pl.ds(0, 8)])
    copy_out(pl.ds(0, BAND))
    copy_out(pl.ds(LOW, BAND))
    landed(stage_6)
    for c in outs:
        c.wait()
    for c in started:
        if not any(c is k for k in ends + rest):
            c.wait_send()


def update_object(canvas, sums, probe, count, obj, east, below, west, above):
    f32 = lambda *d: jax.ShapeDtypeStruct(d, F32)
    vm, any_ = pl.BlockSpec(memory_space=pltpu.VMEM), pl.BlockSpec(memory_space=pl.ANY)
    v = lambda *d: pltpu.VMEM(d, F32)
    small = v(8, H)
    return pl.pallas_call(
        object_kernel,
        out_shape=[f32(2, 7, WIDE, H), f32(6, N, N)],
        in_specs=[any_, vm, vm, vm, any_, any_, any_, any_, any_],
        out_specs=[any_, vm],
        scratch_shapes=[
            v(2, TILES, WIDE, H), v(2, WIDE, H), v(2, WIDE, H),
            v(2, SIDE, H), v(2, SIDE, H), v(2, SIDE, H), v(2, SIDE, H),
            v(2, TILES, H, H), v(2, TILES, H, H), v(2, TILES, 8, H), v(2, TILES, 8, H),
            v(2, 3, H, H), v(2, 3, H, H), v(2, TILES, 8, H), v(2, TILES, 8, H),
            v(2, TILES, SPAN, H), v(2, TILES, SPAN, H), v(2, TILES, WIDE, H), v(TILES, SPAN, H),
            v(2, TILES, EDGE, H), v(2, TILES, EDGE, H), v(2, TILES, EDGE, H), v(TILES, EDGE, H),
            v(2, TILE, H), v(2, TILES, 8, H), v(2, 10, TILES, 8, H), v(2, 2, 16, 8, H), v(16, H),
            v(7, H, N), v(7, H, N), v(2, 3, 7, 32, H), v(2, 7, 32, H), v(2, 3, 7, 8, H), v(2, 7, 8, H),
            v(4, 2, 7, 8, H), small, small, small, small, small,
            pltpu.SemaphoreType.DMA((30,)), pltpu.SemaphoreType.DMA((56,)), pltpu.SemaphoreType.DMA((56,)),
        ],
        compiler_params=pltpu.CompilerParams(
            collective_id=1, has_side_effects=True, vmem_limit_bytes=62 << 20
        ),
    )(canvas, sums, probe, count, obj, east, below, west, above)


def place_kernel(place, parts_in, canvas):
    canvas[...] = jnp.zeros_like(canvas)
    for f in range(parts_in.shape[0]):
        r, c = pl.multiple_of(place[f, 0], H), place[f, 1] // H
        for a in range(2):
            for b in range(2):
                for p in range(2):
                    canvas[p, c + b, pl.ds(r + a * H, H)] += parts_in[f, a, b, p]


def place_frames(place, con):
    vm = pl.BlockSpec(memory_space=pltpu.VMEM)
    return pl.pallas_call(
        place_kernel,
        out_shape=jax.ShapeDtypeStruct((2, 7, WIDE, H), F32),
        in_specs=[pl.BlockSpec(memory_space=pltpu.SMEM), vm],
        out_specs=vm,
        compiler_params=pltpu.CompilerParams(vmem_limit_bytes=40 << 20),
    )(place, con)


def window_kernel(place, field, object_new, patches_new, held, load_sems, sems):
    loads = [pltpu.make_async_copy(field.at[:, t], held.at[:, t], load_sems.at[t]) for t in range(7)]
    for c in loads:
        c.start()
    outs = []
    for t in range(6):
        loads[t].wait()
        outs.append(pltpu.make_async_copy(
            held.at[:, t, pl.ds(0, TILE)], object_new.at[:, :, pl.ds(H * t, H)], sems.at[t]))
        outs[-1].start()
    loads[6].wait()
    for f in range(place.shape[0]):
        r, c = pl.multiple_of(place[f, 0], H), place[f, 1] // H
        for t in range(2):
            outs.append(pltpu.make_async_copy(
                held.at[:, c + t, pl.ds(r, N)], patches_new.at[f, :, :, pl.ds(H * t, H)], sems.at[6 + 2 * f + t]))
            outs[-1].start()
    for c in outs:
        c.wait()


def windows(place, field):
    any_ = pl.BlockSpec(memory_space=pl.ANY)
    f32 = lambda *d: jax.ShapeDtypeStruct(d, F32)
    n = place.shape[0]
    return pl.pallas_call(
        window_kernel,
        out_shape=[f32(2, TILE, TILE), f32(n, 2, N, N)],
        in_specs=[pl.BlockSpec(memory_space=pltpu.SMEM), any_],
        out_specs=[any_, any_],
        scratch_shapes=[
            pltpu.VMEM((2, 7, WIDE, H), F32), pltpu.SemaphoreType.DMA((7,)), pltpu.SemaphoreType.DMA((6 + 2 * n,))],
        compiler_params=pltpu.CompilerParams(vmem_limit_bytes=60 << 20),
    )(place, field)


def per_device(amplitude, patches, dual, probe, obj, positions):
    spot = jnp.stack([lax.axis_index("row"), lax.axis_index("col")]).astype(jnp.int32)
    place = positions - spot * TILE
    dual_new, con, sums, count, *around = frames(place, amplitude, patches, dual, probe, obj)
    canvas = place_frames(place, con)
    field, probe_new = update_object(canvas, sums, probe.reshape(2 * MODES, N, N), count, obj, *around)
    object_new, patches_new = windows(place, field)
    return dual_new, object_new, probe_new.reshape(probe.shape), patches_new


def solution(mesh):
    return jax.shard_map(
        per_device,
        mesh=mesh,
        in_specs=(
            P(("row", "col"), None, None),
            P(("row", "col"), None, None, None),
            P(("row", "col"), None, None, None, None),
            P(),
            P(None, "row", "col"),
            P(("row", "col"), None),
        ),
        out_specs=(
            P(("row", "col"), None, None, None, None),
            P(None, "row", "col"),
            P(),
            P(("row", "col"), None, None, None),
        ),
        check_vma=False,
    )
```
